32 devices in a mesh: op: 4 (over y, core), sec: 8 (over z, x).
Axes of the slice: x: 2, y: 2, z: 4, core: 2. Of those that a mesh axis runs over, the one named last changes fastest.
Arguments:
- psi_first: bfloat16 [32, 256, 256], P('sec'), may hold values from -6 to 6
- psi_second: bfloat16 [32, 256, 256], P('sec'), may hold values from -6 to 6
- left_ops: bfloat16 [1024, 256, 256], P(('op', 'sec')), may hold values from -0.375 to 0.375
- right_ops: bfloat16 [1024, 256, 256], P(('op', 'sec')), may hold values from -0.0625 to 0.0625
- source_local: int32 [1024], P(('op', 'sec')), may hold values from 0 to 3
- target_sector: int32 [1024], P(('op', 'sec')), may hold values from 0 to 31, as said below
Outputs:
- sigma_first: bfloat16 [32, 256, 256], P('sec')
- sigma_second: bfloat16 [32, 256, 256], P('sec')
The draws below stay inside these ranges and needn't reach their ends.
Inputs may be any that keep to these rules, and one draw needn't show every extreme that they name: The 32 terms of one block of the terms name exactly 4 distinct target sectors, no two of them owned by the same index of sec (the same target_sector // 4).
All inputs are finite; a program needn't handle non-finite values.
Results may differ from the reference program's by a relative error of at most 0.0065.
Values may be sent and summed in bfloat16 or wider, within the bound.
No kernel may reach another device: no remote copies, remote signals or barrier semaphores. Data moves between devices by JAX's collectives and lax.ppermute only.
A program may use at most 128 MiB of HBM per device.

```python
import jax
import jax.numpy as jnp
from jax import lax

BLK = 256
SEC_DEV = 4
TERMS_DEV = 32
SECTORS = 32
TERMS = 1024
N_OP = 4
N_SEC = 8


def draw_target_sector(key, part):
    key = jax.random.fold_in(key, 11)
    target_count = min(TERMS_DEV, N_SEC // 2)

    def one_device(device_key):
        key_bias, key_score, key_within, key_rest, key_order = jax.random.split(device_key, 5)
        bias = jax.random.randint(key_bias, (N_SEC,), 0, 3) * 48
        scores = jax.random.randint(key_score, (N_SEC,), 0, 64) + bias
        ordered = jnp.argsort(scores * N_SEC + jnp.arange(N_SEC, dtype=jnp.int32), stable=True)
        holders = ordered[:target_count].astype(jnp.int32)
        within = jax.random.randint(key_within, (target_count,), 0, SEC_DEV)
        targets = holders * SEC_DEV + within
        first = jnp.arange(target_count, dtype=jnp.int32)
        rest = jax.random.randint(key_rest, (TERMS_DEV - target_count,), 0, target_count)
        pick = jnp.concatenate([first, rest.astype(jnp.int32)])
        pick = jax.random.permutation(key_order, pick)
        return targets[pick]
    device_keys = jax.random.split(key, N_OP * N_SEC)
    return jax.vmap(one_device)(device_keys).reshape(-1).astype(jnp.int32)


def touch_ends(entries, rng, least, high):
    longest = entries.shape.index(max(entries.shape))
    spots = []
    for shift in (0, 1):
        where = [jax.random.randint(jax.random.fold_in(rng, axis), (), 0, length) for axis, length in enumerate(entries.shape)]
        where[longest] = (where[longest] + shift) % entries.shape[longest]
        spots.append(tuple(where))
    return entries.at[spots[0]].set(least).at[spots[1]].set(high)


def level_of(stream_key, dims, cuts, least, high):
    def one(dim, shards_of):
        heights = jax.random.uniform(jax.random.fold_in(jax.random.fold_in(stream_key, 6), dim), (shards_of,), jnp.float32, least / len(cuts), high / len(cuts))
        return jnp.repeat(jnp.exp(heights), dims[dim] // shards_of).reshape((-1,) + (1,) * (len(dims) - dim - 1))

    loudness = one(*cuts[0])
    for cut in cuts[1:]:
        loudness = loudness * one(*cut)
    return loudness


def scatter_about(stream_key, extent, deviation, limit, shards=(), held_as=jnp.bfloat16):
    array = jax.random.normal(stream_key, extent, jnp.float32) * deviation
    if len(shards) > 0:
        array = level_of(stream_key, extent, shards, -0.22, 0.18) * array
    return jnp.clip(array, min=-limit, max=limit).astype(held_as)


def setup_inputs(seed: int = 0) -> dict:
    key_of = jax.random.split(jax.random.key(seed), 7)
    psi_first = scatter_about(key_of[0], (SECTORS, BLK, BLK), 1.0, 6.0, ((0, 8),))
    psi_second = scatter_about(key_of[1], (SECTORS, BLK, BLK), 1.0, 6.0, ((0, 8),))
    left_ops = scatter_about(key_of[2], (TERMS, BLK, BLK), BLK ** -0.5, 0.375, ((0, 32),))
    right_ops = scatter_about(key_of[3], (TERMS, BLK, BLK), (BLK * TERMS_DEV * N_OP // SEC_DEV) ** -0.5, 0.0625, ((0, 32),))
    source_local = touch_ends(jax.random.randint(key_of[4], (TERMS,), 0, SEC_DEV), jax.random.fold_in(key_of[4], 1), 0, SEC_DEV - 1).astype(jnp.int32)
    target_sector = draw_target_sector(jax.random.fold_in(key_of[6], 71), 0)
    return dict(psi_first=psi_first, psi_second=psi_second, left_ops=left_ops, right_ops=right_ops, source_local=source_local, target_sector=target_sector)


def reference(psi_first, psi_second, left_ops, right_ops, source_local, target_sector):
    term_ids = jnp.arange(TERMS, dtype=jnp.int32)
    device = term_ids // TERMS_DEV
    source = ((device % N_SEC) * SEC_DEV + source_local).astype(jnp.int32)
    count = N_OP * N_SEC
    pieces = (left_ops.reshape(count, TERMS_DEV, BLK, BLK),
              right_ops.reshape(count, TERMS_DEV, BLK, BLK),
              source.reshape(count, TERMS_DEV),
              target_sector.reshape(count, TERMS_DEV))

    def apply(wavefunction):
        def accumulate(totals, piece):
            left_part, right_part, src, dst = piece
            source_blocks = wavefunction[src].astype(jnp.float32)
            halfway = jnp.einsum('tij,tjk->tik', left_part.astype(jnp.float32), source_blocks).astype(jnp.bfloat16)
            contracted = jnp.einsum('tik,tlk->til', halfway.astype(jnp.float32), right_part.astype(jnp.float32)).astype(jnp.bfloat16)
            local = jnp.zeros((SECTORS, BLK, BLK), jnp.float32).at[dst].add(contracted.astype(jnp.float32))
            totals = totals + local.astype(jnp.bfloat16).astype(jnp.float32)
            return totals, None

        totals, unused = lax.scan(accumulate, jnp.zeros((SECTORS, BLK, BLK), jnp.float32), pieces)
        return totals.astype(jnp.bfloat16)

    return apply(psi_first), apply(psi_second)
```

```python
import functools

import jax
import jax.numpy as jnp
from jax import lax
from jax.experimental import pallas as pl
from jax.experimental.pallas import tpu as pltpu
from jax.sharding import PartitionSpec as P

VMEM_LIMIT = 48 * 1024 * 1024
LABEL_ROWS = 16
AXES = ("op", "sec")


class Plan:
    def __init__(self, mesh, psi, terms):
        self.op, self.sec = mesh.shape["op"], mesh.shape["sec"]
        self.held, self.blk = psi.shape[0], psi.shape[1]
        self.terms = terms
        self.slots = self.sec // 2
        self.extra = 0
        while self.slots * self.op * 2**self.extra < self.held * self.sec:
            self.extra += 1
        self.places = (self.op // 2) * 2**self.extra
        self.rows = self.blk // self.places
        self.bits = list(range(self.extra, self.sec.bit_length() - 1))

    def place(self, op, sec):
        return (op // 2) * 2**self.extra + sec % 2**self.extra

    def swap(self, op_mask, sec_mask):
        n = self.op * self.sec
        mask = op_mask * self.sec + sec_mask
        return [(i, i ^ mask) for i in range(n)]

    def across(self, m):
        return self.swap((m >> self.extra) << 1, m & (2**self.extra - 1))


def contract_kernel(plan, step, src, tgt, left, right, first, second, *rest):
    outs = rest[: plan.places]
    acc, slot_of, labels, seen = rest[plan.places :]
    at = pl.program_id(0)

    @pl.when(at == 0)
    def _():
        for h in range(plan.sec):
            seen[h] = -1

        def name(t, count):
            target = tgt[t]
            holder = target // plan.held
            fresh = seen[holder] < 0
            slot = jnp.where(fresh, count, seen[holder])
            seen[holder] = slot
            labels[slot] = target
            slot_of[t] = slot
            return count + fresh.astype(jnp.int32)

        lax.fori_loop(0, plan.terms, name, jnp.int32(0))
        acc[...] = jnp.zeros_like(acc)

    for i in range(step):
        t = at * step + i
        a = src[t]
        half = [
            jnp.dot(left[i], psi[a], preferred_element_type=jnp.float32).astype(jnp.bfloat16)
            for psi in (first, second)
        ]
        both = jnp.concatenate(half, axis=0)
        acc[slot_of[t]] += lax.dot_general(
            both, right[i], (((1,), (1,)), ((), ())), preferred_element_type=jnp.float32
        )

    @pl.when(at == pl.num_programs(0) - 1)
    def _():
        op, sec = lax.axis_index("op"), lax.axis_index("sec")
        core, place = op % 2, plan.place(op, sec)
        lane = lax.broadcasted_iota(jnp.int32, (LABEL_ROWS, plan.blk), 1)
        tile = jnp.zeros((LABEL_ROWS, plan.blk), jnp.float32)
        for j in range(plan.slots):
            tile = jnp.where(lane == j, labels[j].astype(jnp.float32), tile)
        tile = tile.astype(jnp.bfloat16)
        for m in range(plan.places):
            row = (place ^ m) * plan.rows
            for v in range(2):
                base = pl.multiple_of((core ^ v) * plan.blk + row, plan.rows)
                for j in range(plan.slots):
                    outs[m][pl.ds((v * plan.slots + j) * plan.rows, plan.rows), :] = acc[
                        j, pl.ds(base, plan.rows), :
                    ].astype(jnp.bfloat16)
            outs[m][pl.ds(2 * plan.slots * plan.rows, LABEL_ROWS), :] = tile


def contract(plan, source, target, left, right, first, second):
    step = 4
    blk = plan.blk
    height = 2 * plan.slots * plan.rows + LABEL_ROWS
    whole = pl.BlockSpec((plan.held, blk, blk), lambda t, *_: (0, 0, 0))
    part = pl.BlockSpec((step, blk, blk), lambda t, *_: (t, 0, 0))
    return pl.pallas_call(
        functools.partial(contract_kernel, plan, step),
        grid_spec=pltpu.PrefetchScalarGridSpec(
            num_scalar_prefetch=2,
            grid=(plan.terms // step,),
            in_specs=[part, part, whole, whole],
            out_specs=[pl.BlockSpec((height, blk), lambda t, *_: (0, 0))] * plan.places,
            scratch_shapes=[
                pltpu.VMEM((plan.slots, 2 * blk, blk), jnp.float32),
                pltpu.SMEM((plan.terms,), jnp.int32),
                pltpu.SMEM((plan.slots,), jnp.int32),
                pltpu.SMEM((plan.sec,), jnp.int32),
            ],
        ),
        out_shape=[jax.ShapeDtypeStruct((height, blk), jnp.bfloat16)] * plan.places,
        compiler_params=pltpu.CompilerParams(
            vmem_limit_bytes=VMEM_LIMIT, dimension_semantics=("arbitrary",)
        ),
        name="contract",
    )(source, target, left, right, first, second)


def spread_kernel(plan, want, *refs):
    n = 2 * plan.places
    blocks, tags, out = refs[:n], refs[n : 2 * n], refs[2 * n]
    acc, tags_vector, tags_scalar, sem = refs[2 * n + 1 :]
    for i in range(n):
        row = jnp.max(tags[i][...].astype(jnp.float32), axis=0, keepdims=True)
        tags_vector[pl.ds(i, 1), :] = row[:, :128].astype(jnp.int32)
    copy = pltpu.make_async_copy(tags_vector, tags_scalar, sem)
    copy.start()
    acc[...] = jnp.zeros_like(acc)
    copy.wait()
    sec = lax.axis_index("sec")
    for i in range(n):
        for j in range(plan.slots):
            label = tags_scalar[i, j]
            away = (label // plan.held) ^ sec
            index = jnp.int32(0)
            for b in plan.bits[1:]:
                index = index * 2 + ((away >> b) & 1)
            index = index * 2**plan.extra + (away & (2**plan.extra - 1))
            index = index * plan.held + label % plan.held

            @pl.when(((away >> plan.bits[0]) & 1) == want)
            def _():
                acc[index] += blocks[i][pl.ds(j * plan.rows, plan.rows), :].astype(jnp.float32)

    out[...] = acc[...].astype(jnp.bfloat16).reshape(out.shape)


def spread(plan, want, own, other):
    blk, rows, slots = plan.blk, plan.rows, plan.slots
    sectors = plan.held * 2 ** (plan.extra + len(plan.bits) - 1)
    n = 2 * plan.places

    def half(v):
        return pl.BlockSpec((slots * rows, blk), lambda t: (v, 0))

    tag = pl.BlockSpec((LABEL_ROWS, blk), lambda t: (2 * slots * rows // LABEL_ROWS, 0))
    return pl.pallas_call(
        functools.partial(spread_kernel, plan, want),
        grid=(1,),
        in_specs=[half(0)] * plan.places + [half(1)] * plan.places + [tag] * n,
        out_specs=pl.BlockSpec((sectors * rows, blk), lambda t: (0, 0)),
        out_shape=jax.ShapeDtypeStruct((sectors * rows, blk), jnp.bfloat16),
        scratch_shapes=[
            pltpu.VMEM((sectors, rows, blk), jnp.float32),
            pltpu.VMEM((n, 128), jnp.int32),
            pltpu.SMEM((n, 128), jnp.int32),
            pltpu.SemaphoreType.DMA,
        ],
        compiler_params=pltpu.CompilerParams(vmem_limit_bytes=VMEM_LIMIT),
        name="spread",
    )(*own, *other, *own, *other)


def place_kernel(plan, *refs):
    n = plan.places
    own, other = refs[:n], refs[n : 2 * n]
    outs = refs[2 * n : 2 * n + 2]
    sems = refs[2 * n + 2]
    op, sec = lax.axis_index("op"), lax.axis_index("sec")
    core, place = op % 2, plan.place(op, sec)

    def copies(mine, theirs):
        return [
            pltpu.make_async_copy(
                piece,
                out.at[:, pl.ds(pl.multiple_of((place ^ m) * plan.rows, plan.rows), plan.rows), :],
                sems.at[k, m],
            )
            for k, (pieces, out) in enumerate(((own, mine), (other, theirs)))
            for m, piece in enumerate(pieces)
        ]

    for c in range(2):

        @pl.when(core == c)
        def _():
            moving = copies(outs[c], outs[1 - c])
            for copy in moving:
                copy.start()
            for copy in moving:
                copy.wait()


def assemble(plan, own, other):
    anywhere = pl.BlockSpec(memory_space=pl.ANY)
    result = jax.ShapeDtypeStruct((plan.held, plan.blk, plan.blk), jnp.bfloat16)
    pieces = [x.reshape(plan.held, plan.rows, plan.blk) for x in (*own, *other)]
    return pl.pallas_call(
        functools.partial(place_kernel, plan),
        in_specs=[anywhere] * (2 * plan.places),
        out_specs=[anywhere] * 2,
        out_shape=[result, result],
        scratch_shapes=[pltpu.SemaphoreType.DMA((2, plan.places))],
        name="assemble",
    )(*pieces)


def per_device(mesh, first, second, left, right, source, target):
    plan = Plan(mesh, first, left.shape[0])
    core = plan.swap(1, 0)
    pieces = contract(plan, source, target, left, right, first, second)
    own = list(pieces)
    for m in reversed(range(1, plan.places)):
        own[m] = lax.ppermute(pieces[m], AXES, plan.across(m))
    other = [lax.ppermute(x, AXES, core) for x in own]

    away = spread(plan, 1, own, other)
    kept = spread(plan, 0, own, other)
    total = kept.astype(jnp.float32)
    for k, b in enumerate(plan.bits):
        arrived = lax.ppermute(away, AXES, plan.swap(0, 1 << b))
        total = total + arrived.astype(jnp.float32)
        if k + 1 < len(plan.bits):
            middle = total.shape[0] // 2
            away = total[middle:].astype(jnp.bfloat16)
            total = total[:middle]
    total = total.astype(jnp.bfloat16)

    size = plan.held * plan.rows
    sums = [total[e * size : (e + 1) * size] for e in range(2**plan.extra)]
    own = [sums[m % 2**plan.extra] for m in range(plan.places)]
    for m in reversed(range(1, plan.places)):
        own[m] = lax.ppermute(own[m], AXES, plan.across(m))
    other = [lax.ppermute(x, AXES, core) for x in own]
    return tuple(assemble(plan, own, other))


def solution(mesh):
    in_specs = (
        P("sec", None, None),
        P("sec", None, None),
        P(AXES, None, None),
        P(AXES, None, None),
        P(AXES),
        P(AXES),
    )
    out_specs = (P("sec", None, None), P("sec", None, None))
    return jax.shard_map(
        functools.partial(per_device, mesh),
        mesh=mesh,
        in_specs=in_specs,
        out_specs=out_specs,
        check_vma=False,
    )
```

```python
import functools

import jax
import jax.numpy as jnp
from jax import lax
from jax.experimental import pallas as pl
from jax.experimental.pallas import tpu as pltpu
from jax.sharding import PartitionSpec as P

VMEM_LIMIT = 24 * 1024 * 1024
LABEL_ROWS = 16
AXES = ("op", "sec")


class Plan:
    def __init__(self, mesh, psi, terms):
        self.op, self.sec = mesh.shape["op"], mesh.shape["sec"]
        self.held, self.blk = psi.shape[0], psi.shape[1]
        self.terms = terms
        self.slots = self.sec // 2
        self.extra = 0
        while self.slots * self.op * 2**self.extra < self.held * self.sec:
            self.extra += 1
        self.places = (self.op // 2) * 2**self.extra
        self.rows = self.blk // (2 * self.places)
        self.step = 4
        self.bits = list(range(self.extra, self.sec.bit_length() - 1))

    def place(self, op, sec):
        return (op // 2) * 2**self.extra + sec % 2**self.extra

    def swap(self, op_mask, sec_mask):
        n = self.op * self.sec
        mask = op_mask * self.sec + sec_mask
        return [(i, i ^ mask) for i in range(n)]

    def across(self, m):
        return self.swap((m >> self.extra) << 1, m & (2**self.extra - 1))


def contract_kernel(plan, nv, *refs):
    source, target, left, right = refs[:4]
    vectors = refs[4 : 4 + nv]
    outs = refs[4 + nv : 4 + nv + plan.places]
    src, tgt, lhs, rhs, psi, acc, slot_of, labels, seen, sems, first_sems = refs[4 + nv + plan.places :]
    blk, terms = plan.blk, plan.terms

    heads = [pltpu.make_async_copy(x, y, first_sems.at[i]) for i, (x, y) in enumerate(((target, tgt), (source, src)))]
    heads += [pltpu.make_async_copy(x, psi.at[v], first_sems.at[2 + v]) for v, x in enumerate(vectors)]
    for copy in heads:
        copy.start()

    def loads(c):
        part = pl.ds(c * plan.step, plan.step)
        return [
            pltpu.make_async_copy(left.at[part], lhs.at[part], sems.at[0, c]),
            pltpu.make_async_copy(right.at[part], rhs.at[part], sems.at[1, c]),
        ]

    for c in range(terms // plan.step):
        for copy in loads(c):
            copy.start()
    for h in range(plan.sec):
        seen[h] = -1
    acc[...] = jnp.zeros_like(acc)
    heads[0].wait()

    def name(t, count):
        goal = tgt[t]
        holder = goal // plan.held
        fresh = seen[holder] < 0
        slot = jnp.where(fresh, count, seen[holder])
        seen[holder] = slot
        labels[slot] = goal
        slot_of[t] = slot
        return count + fresh.astype(jnp.int32)

    lax.fori_loop(0, terms, name, jnp.int32(0))
    for copy in heads[1:]:
        copy.wait()

    for t in range(terms):
        if t % plan.step == 0:
            for copy in loads(t // plan.step):
                copy.wait()
        half = [
            jnp.dot(lhs[t], psi[v, src[t]], preferred_element_type=jnp.float32).astype(jnp.bfloat16)
            for v in range(nv)
        ]
        both = jnp.concatenate(half, axis=0) if nv > 1 else half[0]
        acc[slot_of[t]] += lax.dot_general(
            both, rhs[t], (((1,), (1,)), ((), ())), preferred_element_type=jnp.float32
        )

    op, sec = lax.axis_index("op"), lax.axis_index("sec")
    core, place = op % 2, plan.place(op, sec)
    lane = lax.broadcasted_iota(jnp.int32, (LABEL_ROWS, blk), 1)
    tile = jnp.zeros((LABEL_ROWS, blk), jnp.float32)
    for j in range(plan.slots):
        tile = jnp.where(lane == j, labels[j].astype(jnp.float32), tile)
    tile = tile.astype(jnp.bfloat16)
    for m in range(plan.places):
        for rc in range(2):
            row = ((place ^ m) * 2 + (core ^ rc)) * plan.rows
            for v in range(nv):
                base = pl.multiple_of(v * blk + row, plan.rows)
                for j in range(plan.slots):
                    to = ((rc * nv + v) * plan.slots + j) * plan.rows
                    outs[m][pl.ds(to, plan.rows), :] = acc[j, pl.ds(base, plan.rows), :].astype(jnp.bfloat16)
        outs[m][pl.ds(2 * nv * plan.slots * plan.rows, LABEL_ROWS), :] = tile


def contract(plan, source, target, left, right, vectors):
    nv, blk, terms = len(vectors), plan.blk, plan.terms
    height = 2 * nv * plan.slots * plan.rows + LABEL_ROWS
    bf16 = jnp.bfloat16
    arrays = [pltpu.with_memory_space_constraint(x, pltpu.HBM) for x in (source, target, left, right, *vectors)]
    flops = 4 * nv * terms * blk**3
    return pl.pallas_call(
        functools.partial(contract_kernel, plan, nv),
        in_specs=[pl.BlockSpec(memory_space=pltpu.HBM)] * len(arrays),
        out_specs=[pl.BlockSpec(memory_space=pltpu.VMEM)] * plan.places,
        out_shape=[pltpu.VMEM((height, blk), bf16)] * plan.places,
        scratch_shapes=[
            pltpu.SMEM((terms,), jnp.int32),
            pltpu.SMEM((terms,), jnp.int32),
            pltpu.VMEM((terms, blk, blk), bf16),
            pltpu.VMEM((terms, blk, blk), bf16),
            pltpu.VMEM((nv, plan.held, blk, blk), bf16),
            pltpu.VMEM((plan.slots, nv * blk, blk), jnp.float32),
            pltpu.SMEM((terms,), jnp.int32),
            pltpu.SMEM((plan.slots,), jnp.int32),
            pltpu.SMEM((plan.sec,), jnp.int32),
            pltpu.SemaphoreType.DMA((2, terms // plan.step)),
            pltpu.SemaphoreType.DMA((2 + nv,)),
        ],
        cost_estimate=pl.CostEstimate(flops=flops, bytes_accessed=4 * terms * blk * blk, transcendentals=0),
        compiler_params=pltpu.CompilerParams(vmem_limit_bytes=VMEM_LIMIT),
        name="contract",
    )(*arrays)


def spread_kernel(plan, nv, want, *refs):
    n = 2 * plan.places
    blocks, tags, out = refs[:n], refs[n : 2 * n], refs[2 * n]
    acc, tags_vector, tags_scalar, sem = refs[2 * n + 1 :]
    for i in range(n):
        row = jnp.max(tags[i][...].astype(jnp.float32), axis=0, keepdims=True)
        tags_vector[pl.ds(i, 1), :] = row[:, :128].astype(jnp.int32)
    copy = pltpu.make_async_copy(tags_vector, tags_scalar, sem)
    copy.start()
    acc[...] = jnp.zeros_like(acc)
    copy.wait()
    sec = lax.axis_index("sec")
    for i in range(n):
        for j in range(plan.slots):
            label = tags_scalar[i, j]
            away = (label // plan.held) ^ sec
            index = jnp.int32(0)
            for b in plan.bits[1:]:
                index = index * 2 + ((away >> b) & 1)
            index = index * 2**plan.extra + (away & (2**plan.extra - 1))

            @pl.when(((away >> plan.bits[0]) & 1) == want)
            def _():
                for v in range(nv):
                    block = blocks[i][pl.ds((v * plan.slots + j) * plan.rows, plan.rows), :]
                    acc[(index * nv + v) * plan.held + label % plan.held] += block.astype(jnp.float32)

    out[...] = acc[...].astype(jnp.bfloat16).reshape(out.shape)


def spread(plan, nv, want, own, other):
    blk, rows, slots = plan.blk, plan.rows, plan.slots
    sectors = nv * plan.held * 2 ** (plan.extra + len(plan.bits) - 1)
    n = 2 * plan.places

    def half(rc):
        return pl.BlockSpec((nv * slots * rows, blk), lambda t: (rc, 0))

    tag = pl.BlockSpec((LABEL_ROWS, blk), lambda t: (2 * nv * slots * rows // LABEL_ROWS, 0))
    return pl.pallas_call(
        functools.partial(spread_kernel, plan, nv, want),
        grid=(1,),
        in_specs=[half(0)] * plan.places + [half(1)] * plan.places + [tag] * n,
        out_specs=pl.BlockSpec((sectors * rows, blk), lambda t: (0, 0)),
        out_shape=jax.ShapeDtypeStruct((sectors * rows, blk), jnp.bfloat16),
        scratch_shapes=[
            pltpu.VMEM((sectors, rows, blk), jnp.float32),
            pltpu.VMEM((n, 128), jnp.int32),
            pltpu.SMEM((n, 128), jnp.int32),
            pltpu.SemaphoreType.DMA,
        ],
        compiler_params=pltpu.CompilerParams(vmem_limit_bytes=VMEM_LIMIT),
        name="spread",
    )(*own, *other, *own, *other)


def place_kernel(plan, nv, *refs):
    n = 2 * plan.places
    pieces, outs, sems = refs[:n], refs[n : n + nv], refs[n + nv]
    op, sec = lax.axis_index("op"), lax.axis_index("sec")
    core, place = op % 2, plan.place(op, sec)
    moving = []
    for i, piece in enumerate(pieces):
        rc, m = divmod(i, plan.places)
        row = pl.multiple_of(((place ^ m) * 2 + (core ^ rc)) * plan.rows, plan.rows)
        for v in range(nv):
            moving.append(pltpu.make_async_copy(piece.at[v], outs[v].at[:, pl.ds(row, plan.rows), :], sems.at[i, v]))
    for copy in moving:
        copy.start()
    for copy in moving:
        copy.wait()


def assemble(plan, nv, own, other):
    result = jax.ShapeDtypeStruct((plan.held, plan.blk, plan.blk), jnp.bfloat16)
    pieces = [
        pltpu.with_memory_space_constraint(x.reshape(nv, plan.held, plan.rows, plan.blk), pltpu.VMEM)
        for x in (*own, *other)
    ]
    return pl.pallas_call(
        functools.partial(place_kernel, plan, nv),
        in_specs=[pl.BlockSpec(memory_space=pltpu.VMEM)] * len(pieces),
        out_specs=[pl.BlockSpec(memory_space=pl.ANY)] * nv,
        out_shape=[result] * nv,
        scratch_shapes=[pltpu.SemaphoreType.DMA((len(pieces), nv))],
        compiler_params=pltpu.CompilerParams(vmem_limit_bytes=VMEM_LIMIT),
        name="assemble",
    )(*pieces)


def exchange(plan, pieces):
    own = list(pieces)
    for m in reversed(range(1, plan.places)):
        own[m] = lax.ppermute(pieces[m], AXES, plan.across(m))
    other = [lax.ppermute(x, AXES, plan.swap(1, 0)) for x in own]
    return own, other


def combine(plan, nv, pieces):
    own, other = exchange(plan, pieces)
    away = spread(plan, nv, 1, own, other)
    kept = spread(plan, nv, 0, own, other)
    total = kept.astype(jnp.float32)
    for k, b in enumerate(plan.bits):
        arrived = lax.ppermute(away, AXES, plan.swap(0, 1 << b))
        total = total + arrived.astype(jnp.float32)
        if k + 1 < len(plan.bits):
            middle = total.shape[0] // 2
            away = total[middle:].astype(jnp.bfloat16)
            total = total[:middle]
    total = total.astype(jnp.bfloat16)
    size = nv * plan.held * plan.rows
    sums = [total[e * size : (e + 1) * size] for e in range(2**plan.extra)]
    own, other = exchange(plan, [sums[m % 2**plan.extra] for m in range(plan.places)])
    return assemble(plan, nv, own, other)


def per_device(mesh, groups, first, second, left, right, source, target):
    plan = Plan(mesh, first, left.shape[0])
    vectors = (first, second)
    results = []
    for group in groups:
        pieces = contract(plan, source, target, left, right, [vectors[v] for v in group])
        results += combine(plan, len(group), pieces)
    return tuple(results)


def solution(mesh):
    in_specs = (
        P("sec", None, None),
        P("sec", None, None),
        P(AXES, None, None),
        P(AXES, None, None),
        P(AXES),
        P(AXES),
    )
    out_specs = (P("sec", None, None), P("sec", None, None))
    return jax.shard_map(
        functools.partial(per_device, mesh, ((0,), (1,))),
        mesh=mesh,
        in_specs=in_specs,
        out_specs=out_specs,
        check_vma=False,
    )
```

```python
import functools

import jax
import jax.numpy as jnp
from jax import lax
from jax.experimental import pallas as pl
from jax.experimental.pallas import tpu as pltpu
from jax.sharding import PartitionSpec as P

VMEM_LIMIT = 16 * 1024 * 1024
LABEL_ROWS = 16
AXES = ("op", "sec")


class Plan:
    def __init__(self, mesh, psi, terms):
        self.op, self.sec = mesh.shape["op"], mesh.shape["sec"]
        self.held, self.blk = psi.shape[0], psi.shape[1]
        self.terms = terms
        self.slots = self.sec // 2
        self.extra = 0
        while self.slots * self.op * 2**self.extra < self.held * self.sec:
            self.extra += 1
        self.places = (self.op // 2) * 2**self.extra
        self.rows = self.blk // (2 * self.places)
        self.step, self.window = 2, 6
        self.bits = list(range(self.extra, self.sec.bit_length() - 1))

    def place(self, op, sec):
        return (op // 2) * 2**self.extra + sec % 2**self.extra

    def swap(self, op_mask, sec_mask):
        n = self.op * self.sec
        mask = op_mask * self.sec + sec_mask
        return [(i, i ^ mask) for i in range(n)]

    def across(self, m):
        return self.swap((m >> self.extra) << 1, m & (2**self.extra - 1))


def contract_kernel(plan, fetch, *refs):
    source, target, left, right, vector = refs[:5]
    outs, refs = refs[5 : 5 + plan.places], refs[5 + plan.places :]
    if fetch:
        lhs, rhs, refs = refs[0], refs[1], refs[2:]
    else:
        lhs, rhs = left, right
    src, tgt, psi, acc, slot_of, labels, seen, sems, first_sems = refs
    blk, terms, step = plan.blk, plan.terms, plan.step
    chunks = terms // step if fetch else 0

    heads = [
        pltpu.make_async_copy(x, y, first_sems.at[i])
        for i, (x, y) in enumerate(((target, tgt), (source, src), (vector, psi)))
    ]
    for copy in heads:
        copy.start()

    def loads(c):
        part = pl.ds(c * step, step)
        return [
            pltpu.make_async_copy(left.at[part], lhs.at[part], sems.at[0, c]),
            pltpu.make_async_copy(right.at[part], rhs.at[part], sems.at[1, c]),
        ]

    def begin(c):
        if c < chunks:
            for copy in loads(c):
                copy.start()

    for c in range(plan.window):
        begin(c)
    for h in range(plan.sec):
        seen[h] = -1
    acc[...] = jnp.zeros_like(acc)
    heads[0].wait()

    def name(t, count):
        goal = tgt[t]
        holder = goal // plan.held
        fresh = seen[holder] < 0
        slot = jnp.where(fresh, count, seen[holder])
        seen[holder] = slot
        labels[slot] = goal
        slot_of[t] = slot
        return count + fresh.astype(jnp.int32)

    lax.fori_loop(0, terms, name, jnp.int32(0))
    for copy in heads[1:]:
        copy.wait()

    for t in range(terms):
        if fetch and t % step == 0:
            for copy in loads(t // step):
                copy.wait()
            begin(t // step + plan.window)
        half = jnp.dot(lhs[t], psi[src[t]], preferred_element_type=jnp.float32).astype(jnp.bfloat16)
        acc[slot_of[t]] += lax.dot_general(
            half, rhs[t], (((1,), (1,)), ((), ())), preferred_element_type=jnp.float32
        )

    op, sec = lax.axis_index("op"), lax.axis_index("sec")
    core, place = op % 2, plan.place(op, sec)
    lane = lax.broadcasted_iota(jnp.int32, (LABEL_ROWS, blk), 1)
    tile = jnp.zeros((LABEL_ROWS, blk), jnp.float32)
    for j in range(plan.slots):
        tile = jnp.where(lane == j, labels[j].astype(jnp.float32), tile)
    tile = tile.astype(jnp.bfloat16)
    for m in range(plan.places):
        for rc in range(2):
            row = pl.multiple_of(((place ^ m) * 2 + (core ^ rc)) * plan.rows, plan.rows)
            for j in range(plan.slots):
                to = (rc * plan.slots + j) * plan.rows
                outs[m][pl.ds(to, plan.rows), :] = acc[j, pl.ds(row, plan.rows), :].astype(jnp.bfloat16)
        outs[m][pl.ds(2 * plan.slots * plan.rows, LABEL_ROWS), :] = tile


def contract(plan, fetch, source, target, left, right, vector):
    blk, terms = plan.blk, plan.terms
    height = 2 * plan.slots * plan.rows + LABEL_ROWS
    bf16 = jnp.bfloat16
    spaces = [pltpu.HBM, pltpu.HBM, *[pltpu.HBM if fetch else pltpu.VMEM] * 2, pltpu.HBM]
    arrays = [
        pltpu.with_memory_space_constraint(x, space)
        for x, space in zip((source, target, left, right, vector), spaces)
    ]
    out_shape = [pltpu.VMEM((height, blk), bf16)] * plan.places
    if fetch:
        out_shape += [pltpu.VMEM((terms, blk, blk), bf16)] * 2
    return pl.pallas_call(
        functools.partial(contract_kernel, plan, fetch),
        in_specs=[pl.BlockSpec(memory_space=space) for space in spaces],
        out_specs=[pl.BlockSpec(memory_space=pltpu.VMEM)] * len(out_shape),
        out_shape=out_shape,
        scratch_shapes=[
            pltpu.SMEM((terms,), jnp.int32),
            pltpu.SMEM((terms,), jnp.int32),
            pltpu.VMEM((plan.held, blk, blk), bf16),
            pltpu.VMEM((plan.slots, blk, blk), jnp.float32),
            pltpu.SMEM((terms,), jnp.int32),
            pltpu.SMEM((plan.slots,), jnp.int32),
            pltpu.SMEM((plan.sec,), jnp.int32),
            pltpu.SemaphoreType.DMA((2, terms // plan.step)),
            pltpu.SemaphoreType.DMA((3,)),
        ],
        cost_estimate=pl.CostEstimate(
            flops=4 * terms * blk**3,
            bytes_accessed=4 * terms * blk * blk if fetch else terms * blk,
            transcendentals=0,
        ),
        compiler_params=pltpu.CompilerParams(vmem_limit_bytes=VMEM_LIMIT),
        name="contract",
    )(*arrays)


def spread_kernel(plan, *refs):
    n = 2 * plan.places
    blocks, tags, outs = refs[:n], refs[n : 2 * n], refs[2 * n : 2 * n + 2]
    acc, tags_vector, tags_scalar, sem = refs[2 * n + 2 :]
    for i in range(n):
        row = jnp.max(tags[i][...].astype(jnp.float32), axis=0, keepdims=True)
        tags_vector[pl.ds(i, 1), :] = row[:, :128].astype(jnp.int32)
    copy = pltpu.make_async_copy(tags_vector, tags_scalar, sem)
    copy.start()
    acc[...] = jnp.zeros_like(acc)
    copy.wait()
    sec = lax.axis_index("sec")
    for i in range(n):
        for j in range(plan.slots):
            label = tags_scalar[i, j]
            away = (label // plan.held) ^ sec
            index = jnp.int32(0)
            for b in plan.bits:
                index = index * 2 + ((away >> b) & 1)
            index = index * 2**plan.extra + (away & (2**plan.extra - 1))
            acc[index * plan.held + label % plan.held] += blocks[i][pl.ds(j * plan.rows, plan.rows), :].astype(jnp.float32)
    half = acc.shape[0] // 2
    for k, out in enumerate(outs):
        out[...] = acc[pl.ds((1 - k) * half, half)].astype(jnp.bfloat16).reshape(out.shape)


def spread(plan, own, other):
    blk, rows, slots = plan.blk, plan.rows, plan.slots
    sectors = plan.held * 2 ** (plan.extra + len(plan.bits))
    n = 2 * plan.places

    def half(rc):
        return pl.BlockSpec((slots * rows, blk), lambda t: (rc, 0))

    tag = pl.BlockSpec((LABEL_ROWS, blk), lambda t: (2 * slots * rows // LABEL_ROWS, 0))
    height = sectors // 2 * rows
    return pl.pallas_call(
        functools.partial(spread_kernel, plan),
        grid=(1,),
        in_specs=[half(0)] * plan.places + [half(1)] * plan.places + [tag] * n,
        out_specs=[pl.BlockSpec((height, blk), lambda t: (0, 0))] * 2,
        out_shape=[jax.ShapeDtypeStruct((height, blk), jnp.bfloat16)] * 2,
        scratch_shapes=[
            pltpu.VMEM((sectors, rows, blk), jnp.float32),
            pltpu.VMEM((n, 128), jnp.int32),
            pltpu.SMEM((n, 128), jnp.int32),
            pltpu.SemaphoreType.DMA,
        ],
        compiler_params=pltpu.CompilerParams(vmem_limit_bytes=VMEM_LIMIT),
        name="spread",
    )(*own, *other, *own, *other)


def place_kernel(plan, *refs):
    n = 2 * plan.places
    pieces, out, sems = refs[:n], refs[n], refs[n + 1]
    op, sec = lax.axis_index("op"), lax.axis_index("sec")
    core, place = op % 2, plan.place(op, sec)
    moving = []
    for i, piece in enumerate(pieces):
        rc, m = divmod(i, plan.places)
        row = pl.multiple_of(((place ^ m) * 2 + (core ^ rc)) * plan.rows, plan.rows)
        moving.append(pltpu.make_async_copy(piece, out.at[:, pl.ds(row, plan.rows), :], sems.at[i]))
    for copy in moving:
        copy.start()
    for copy in moving:
        copy.wait()


def assemble(plan, own, other):
    pieces = [
        pltpu.with_memory_space_constraint(x.reshape(plan.held, plan.rows, plan.blk), pltpu.VMEM)
        for x in (*own, *other)
    ]
    return pl.pallas_call(
        functools.partial(place_kernel, plan),
        in_specs=[pl.BlockSpec(memory_space=pltpu.VMEM)] * len(pieces),
        out_specs=pl.BlockSpec(memory_space=pl.ANY),
        out_shape=jax.ShapeDtypeStruct((plan.held, plan.blk, plan.blk), jnp.bfloat16),
        scratch_shapes=[pltpu.SemaphoreType.DMA((len(pieces),))],
        compiler_params=pltpu.CompilerParams(vmem_limit_bytes=VMEM_LIMIT),
        name="assemble",
    )(*pieces)


def across(plan, pieces):
    own = list(pieces)
    for m in reversed(range(1, plan.places)):
        own[m] = lax.ppermute(pieces[m], AXES, plan.across(m))
    return own


def to_core(plan, own):
    return [lax.ppermute(x, AXES, plan.swap(1, 0)) for x in own]


def combine(plan, own):
    away, kept = spread(plan, own, to_core(plan, own))
    total = kept.astype(jnp.float32)
    for k, b in enumerate(plan.bits):
        arrived = lax.ppermute(away, AXES, plan.swap(0, 1 << b))
        total = total + arrived.astype(jnp.float32)
        if k + 1 < len(plan.bits):
            middle = total.shape[0] // 2
            away = total[middle:].astype(jnp.bfloat16)
            total = total[:middle]
    total = total.astype(jnp.bfloat16)
    size = plan.held * plan.rows
    sums = [total[e * size : (e + 1) * size] for e in range(2**plan.extra)]
    own = across(plan, [sums[m % 2**plan.extra] for m in range(plan.places)])
    return assemble(plan, own, to_core(plan, own))


def per_device(mesh, first, second, left, right, source, target):
    plan = Plan(mesh, first, left.shape[0])
    *pieces, lhs, rhs = contract(plan, True, source, target, left, right, first)
    early = across(plan, pieces)
    pieces = contract(plan, False, source, target, lhs, rhs, second)
    early, pieces = lax.optimization_barrier((early, pieces))
    late = across(plan, pieces)
    return combine(plan, early), combine(plan, late)


def solution(mesh):
    in_specs = (
        P("sec", None, None),
        P("sec", None, None),
        P(AXES, None, None),
        P(AXES, None, None),
        P(AXES),
        P(AXES),
    )
    out_specs = (P("sec", None, None), P("sec", None, None))
    return jax.shard_map(
        functools.partial(per_device, mesh),
        mesh=mesh,
        in_specs=in_specs,
        out_specs=out_specs,
        check_vma=False,
    )
```

```python
import functools

import jax
import jax.numpy as jnp
from jax import lax
from jax.experimental import pallas as pl
from jax.experimental.pallas import tpu as pltpu
from jax.sharding import PartitionSpec as P

VMEM_LIMIT = 16 * 1024 * 1024
LABEL_ROWS = 16
AXES = ("op", "sec")


class Plan:
    def __init__(self, mesh, psi, terms, order):
        self.op, self.sec = mesh.shape["op"], mesh.shape["sec"]
        self.held, self.blk = psi.shape[0], psi.shape[1]
        self.terms = terms
        self.slots = self.sec // 2
        extra = 0
        while self.slots * self.op * 2**extra < self.held * self.sec:
            extra += 1
        self.inside, self.bits = order[:extra], order[extra:]
        self.places = (self.op // 2) * 2**extra
        self.rows = self.blk // (2 * self.places)
        self.step, self.window = 8, 2

    def extra(self, sec):
        total = sec * 0
        for i, b in enumerate(self.inside):
            total = total + (((sec >> b) & 1) << i)
        return total

    def place(self, op, sec):
        return (op // 2) * 2 ** len(self.inside) + self.extra(sec)

    def swap(self, op_mask, sec_mask):
        n = self.op * self.sec
        mask = op_mask * self.sec + sec_mask
        return [(i, i ^ mask) for i in range(n)]

    def across(self, m):
        sec_mask = sum(((m >> i) & 1) << b for i, b in enumerate(self.inside))
        return self.swap((m >> len(self.inside)) << 1, sec_mask)


def contract_kernel(plan, fetch, *refs):
    source, target, left, right, vector = refs[:5]
    outs, refs = refs[5 : 5 + plan.places], refs[5 + plan.places :]
    if fetch:
        lhs, rhs, refs = refs[0], refs[1], refs[2:]
    else:
        lhs, rhs = left, right
    src, tgt, psi, acc, slot_of, labels, seen, sems, first_sems = refs
    blk, terms, step = plan.blk, plan.terms, plan.step
    chunks = terms // step if fetch else 0

    heads = [
        pltpu.make_async_copy(x, y, first_sems.at[i])
        for i, (x, y) in enumerate(((target, tgt), (source, src), (vector, psi)))
    ]
    for copy in heads:
        copy.start()

    def loads(c):
        part = pl.ds(c * step, step)
        return [
            pltpu.make_async_copy(left.at[part], lhs.at[part], sems.at[0, c]),
            pltpu.make_async_copy(right.at[part], rhs.at[part], sems.at[1, c]),
        ]

    def begin(c):
        if c < chunks:
            for copy in loads(c):
                copy.start()

    for c in range(plan.window):
        begin(c)
    for h in range(plan.sec):
        seen[h] = -1
    acc[...] = jnp.zeros_like(acc)
    heads[0].wait()

    def name(t, count):
        goal = tgt[t]
        holder = goal // plan.held
        fresh = seen[holder] < 0
        slot = jnp.where(fresh, count, seen[holder])
        seen[holder] = slot
        labels[slot] = goal
        slot_of[t] = slot
        return count + fresh.astype(jnp.int32)

    lax.fori_loop(0, terms, name, jnp.int32(0))
    for copy in heads[1:]:
        copy.wait()

    for t in range(terms):
        if fetch and t % step == 0:
            for copy in loads(t // step):
                copy.wait()
            begin(t // step + plan.window)
        half = jnp.dot(lhs[t], psi[src[t]], preferred_element_type=jnp.float32).astype(jnp.bfloat16)
        acc[slot_of[t]] += lax.dot_general(
            half, rhs[t], (((1,), (1,)), ((), ())), preferred_element_type=jnp.float32
        )

    op, sec = lax.axis_index("op"), lax.axis_index("sec")
    core, place = op % 2, plan.place(op, sec)
    lane = lax.broadcasted_iota(jnp.int32, (LABEL_ROWS, blk), 1)
    tile = jnp.zeros((LABEL_ROWS, blk), jnp.float32)
    for j in range(plan.slots):
        tile = jnp.where(lane == j, labels[j].astype(jnp.float32), tile)
    tile = tile.astype(jnp.bfloat16)
    for m in range(plan.places):
        for rc in range(2):
            row = pl.multiple_of(((place ^ m) * 2 + (core ^ rc)) * plan.rows, plan.rows)
            for j in range(plan.slots):
                to = (rc * plan.slots + j) * plan.rows
                outs[m][pl.ds(to, plan.rows), :] = acc[j, pl.ds(row, plan.rows), :].astype(jnp.bfloat16)
        outs[m][pl.ds(2 * plan.slots * plan.rows, LABEL_ROWS), :] = tile


def contract(plan, fetch, source, target, left, right, vector):
    blk, terms = plan.blk, plan.terms
    height = 2 * plan.slots * plan.rows + LABEL_ROWS
    bf16 = jnp.bfloat16
    spaces = [pltpu.HBM, pltpu.HBM, *[pltpu.HBM if fetch else pltpu.VMEM] * 2, pltpu.HBM]
    arrays = [
        pltpu.with_memory_space_constraint(x, space)
        for x, space in zip((source, target, left, right, vector), spaces)
    ]
    out_shape = [pltpu.VMEM((height, blk), bf16)] * plan.places
    if fetch:
        out_shape += [pltpu.VMEM((terms, blk, blk), bf16)] * 2
    return pl.pallas_call(
        functools.partial(contract_kernel, plan, fetch),
        in_specs=[pl.BlockSpec(memory_space=space) for space in spaces],
        out_specs=[pl.BlockSpec(memory_space=pltpu.VMEM)] * len(out_shape),
        out_shape=out_shape,
        scratch_shapes=[
            pltpu.SMEM((terms,), jnp.int32),
            pltpu.SMEM((terms,), jnp.int32),
            pltpu.VMEM((plan.held, blk, blk), bf16),
            pltpu.VMEM((plan.slots, blk, blk), jnp.float32),
            pltpu.SMEM((terms,), jnp.int32),
            pltpu.SMEM((plan.slots,), jnp.int32),
            pltpu.SMEM((plan.sec,), jnp.int32),
            pltpu.SemaphoreType.DMA((2, terms // plan.step)),
            pltpu.SemaphoreType.DMA((3,)),
        ],
        cost_estimate=pl.CostEstimate(
            flops=4 * terms * blk**3,
            bytes_accessed=4 * terms * blk * blk if fetch else terms * blk,
            transcendentals=0,
        ),
        compiler_params=pltpu.CompilerParams(vmem_limit_bytes=VMEM_LIMIT),
        name="contract",
    )(*arrays)


def spread_kernel(plan, *refs):
    n = 2 * plan.places
    blocks, tags, outs = refs[:n], refs[n : 2 * n], refs[2 * n : 2 * n + 2]
    acc, tags_vector, tags_scalar, sem = refs[2 * n + 2 :]
    for i in range(n):
        row = jnp.max(tags[i][...].astype(jnp.float32), axis=0, keepdims=True)
        tags_vector[pl.ds(i, 1), :] = row[:, :128].astype(jnp.int32)
    copy = pltpu.make_async_copy(tags_vector, tags_scalar, sem)
    copy.start()
    acc[...] = jnp.zeros_like(acc)
    copy.wait()
    sec = lax.axis_index("sec")
    for i in range(n):
        for j in range(plan.slots):
            label = tags_scalar[i, j]
            away = (label // plan.held) ^ sec
            index = jnp.int32(0)
            for b in plan.bits:
                index = index * 2 + ((away >> b) & 1)
            index = index * 2 ** len(plan.inside) + plan.extra(away)
            acc[index * plan.held + label % plan.held] += blocks[i][pl.ds(j * plan.rows, plan.rows), :].astype(jnp.float32)
    half = acc.shape[0] // 2
    for k, out in enumerate(outs):
        out[...] = acc[pl.ds((1 - k) * half, half)].astype(jnp.bfloat16).reshape(out.shape)


def spread(plan, own, other):
    blk, rows, slots = plan.blk, plan.rows, plan.slots
    sectors = plan.held * plan.sec
    n = 2 * plan.places

    def half(rc):
        return pl.BlockSpec((slots * rows, blk), lambda t: (rc, 0))

    tag = pl.BlockSpec((LABEL_ROWS, blk), lambda t: (2 * slots * rows // LABEL_ROWS, 0))
    height = sectors // 2 * rows
    return pl.pallas_call(
        functools.partial(spread_kernel, plan),
        grid=(1,),
        in_specs=[half(0)] * plan.places + [half(1)] * plan.places + [tag] * n,
        out_specs=[pl.BlockSpec((height, blk), lambda t: (0, 0))] * 2,
        out_shape=[jax.ShapeDtypeStruct((height, blk), jnp.bfloat16)] * 2,
        scratch_shapes=[
            pltpu.VMEM((sectors, rows, blk), jnp.float32),
            pltpu.VMEM((n, 128), jnp.int32),
            pltpu.SMEM((n, 128), jnp.int32),
            pltpu.SemaphoreType.DMA,
        ],
        compiler_params=pltpu.CompilerParams(vmem_limit_bytes=VMEM_LIMIT),
        name="spread",
    )(*own, *other, *own, *other)


def place_kernel(plan, *refs):
    n = 2 * plan.places
    pieces, out, sems = refs[:n], refs[n], refs[n + 1]
    op, sec = lax.axis_index("op"), lax.axis_index("sec")
    core, place = op % 2, plan.place(op, sec)
    moving = []
    for i, piece in enumerate(pieces):
        rc, m = divmod(i, plan.places)
        row = pl.multiple_of(((place ^ m) * 2 + (core ^ rc)) * plan.rows, plan.rows)
        moving.append(pltpu.make_async_copy(piece, out.at[:, pl.ds(row, plan.rows), :], sems.at[i]))
    for copy in moving:
        copy.start()
    for copy in moving:
        copy.wait()


def assemble(plan, own, other):
    pieces = [
        pltpu.with_memory_space_constraint(x.reshape(plan.held, plan.rows, plan.blk), pltpu.VMEM)
        for x in (*own, *other)
    ]
    return pl.pallas_call(
        functools.partial(place_kernel, plan),
        in_specs=[pl.BlockSpec(memory_space=pltpu.VMEM)] * len(pieces),
        out_specs=pl.BlockSpec(memory_space=pl.ANY),
        out_shape=jax.ShapeDtypeStruct((plan.held, plan.blk, plan.blk), jnp.bfloat16),
        scratch_shapes=[pltpu.SemaphoreType.DMA((len(pieces),))],
        compiler_params=pltpu.CompilerParams(vmem_limit_bytes=VMEM_LIMIT),
        name="assemble",
    )(*pieces)


def across(plan, pieces):
    own = list(pieces)
    for m in reversed(range(1, plan.places)):
        own[m] = lax.ppermute(pieces[m], AXES, plan.across(m))
    return own


def to_core(plan, own):
    return [lax.ppermute(x, AXES, plan.swap(1, 0)) for x in own]


def finish(plan, away, kept):
    total = kept.astype(jnp.float32)
    for k, b in enumerate(plan.bits):
        arrived = lax.ppermute(away, AXES, plan.swap(0, 1 << b))
        total = total + arrived.astype(jnp.float32)
        if k + 1 < len(plan.bits):
            middle = total.shape[0] // 2
            away = total[middle:].astype(jnp.bfloat16)
            total = total[:middle]
    total = total.astype(jnp.bfloat16)
    size = plan.held * plan.rows
    extras = 2 ** len(plan.inside)
    sums = [total[e * size : (e + 1) * size] for e in range(extras)]
    own = across(plan, [sums[m % extras] for m in range(plan.places)])
    return assemble(plan, own, to_core(plan, own))


def per_device(mesh, first, second, left, right, source, target):
    terms = left.shape[0]
    order = list(range(mesh.shape["sec"].bit_length() - 1))
    plan = Plan(mesh, first, terms, order)
    other_plan = Plan(mesh, first, terms, [order[1], order[0], *order[2:]])

    *pieces, lhs, rhs = contract(plan, True, source, target, left, right, first)
    early = across(plan, pieces)
    pieces = contract(other_plan, False, source, target, lhs, rhs, second)
    early, pieces = lax.optimization_barrier((early, pieces))
    late = across(other_plan, pieces)
    away, kept = spread(plan, early, to_core(plan, early))
    away, late = lax.optimization_barrier((away, late))
    result = finish(plan, away, kept)
    return result, finish(other_plan, *spread(other_plan, late, to_core(other_plan, late)))


def solution(mesh):
    in_specs = (
        P("sec", None, None),
        P("sec", None, None),
        P(AXES, None, None),
        P(AXES, None, None),
        P(AXES),
        P(AXES),
    )
    out_specs = (P("sec", None, None), P("sec", None, None))
    return jax.shard_map(
        functools.partial(per_device, mesh),
        mesh=mesh,
        in_specs=in_specs,
        out_specs=out_specs,
        check_vma=False,
    )
```

```python
import functools

import jax
import jax.numpy as jnp
from jax import lax
from jax.experimental import pallas as pl
from jax.experimental.pallas import tpu as pltpu
from jax.sharding import PartitionSpec as P

VMEM_LIMIT = 16 * 1024 * 1024
LABEL_ROWS = 16
AXES = ("op", "sec")


class Plan:
    def __init__(self, mesh, psi, terms, order):
        self.op, self.sec = mesh.shape["op"], mesh.shape["sec"]
        self.held, self.blk = psi.shape[0], psi.shape[1]
        self.terms = terms
        self.slots = self.sec // 2
        extra = 0
        while self.slots * self.op * 2**extra < self.held * self.sec:
            extra += 1
        self.inside, self.bits = order[:extra], order[extra:]
        self.places = (self.op // 2) * 2**extra
        self.rows = self.blk // (2 * self.places)
        self.step, self.window = 8, 2

    def extra(self, sec):
        total = sec * 0
        for i, b in enumerate(self.inside):
            total = total + (((sec >> b) & 1) << i)
        return total

    def place(self, op, sec):
        return (op // 2) * 2 ** len(self.inside) + self.extra(sec)

    def swap(self, op_mask, sec_mask):
        n = self.op * self.sec
        mask = op_mask * self.sec + sec_mask
        return [(i, i ^ mask) for i in range(n)]

    def across(self, m):
        sec_mask = sum(((m >> i) & 1) << b for i, b in enumerate(self.inside))
        return self.swap((m >> len(self.inside)) << 1, sec_mask)


def contract_kernel(plan, fetch, *refs):
    source, target, left, right, vector = refs[:5]
    outs, refs = refs[5 : 5 + plan.places], refs[5 + plan.places :]
    if fetch:
        lhs, rhs, refs = refs[0], refs[1], refs[2:]
    else:
        lhs, rhs = left, right
    src, tgt, psi, acc, slot_of, labels, seen, sems, first_sems = refs
    blk, terms, step = plan.blk, plan.terms, plan.step
    chunks = terms // step if fetch else 0

    heads = [
        pltpu.make_async_copy(x, y, first_sems.at[i])
        for i, (x, y) in enumerate(((target, tgt), (source, src), (vector, psi)))
    ]
    for copy in heads:
        copy.start()

    def loads(c):
        part = pl.ds(c * step, step)
        return [
            pltpu.make_async_copy(left.at[part], lhs.at[part], sems.at[0, c]),
            pltpu.make_async_copy(right.at[part], rhs.at[part], sems.at[1, c]),
        ]

    def begin(c):
        if c < chunks:
            for copy in loads(c):
                copy.start()

    for c in range(plan.window):
        begin(c)
    for h in range(plan.sec):
        seen[h] = -1
    acc[...] = jnp.zeros_like(acc)
    heads[0].wait()

    def name(t, count):
        goal = tgt[t]
        holder = goal // plan.held
        fresh = seen[holder] < 0
        slot = jnp.where(fresh, count, seen[holder])
        seen[holder] = slot
        labels[slot] = goal
        slot_of[t] = slot
        return count + fresh.astype(jnp.int32)

    lax.fori_loop(0, terms, name, jnp.int32(0))
    for copy in heads[1:]:
        copy.wait()

    for t in range(terms):
        if fetch and t % step == 0:
            for copy in loads(t // step):
                copy.wait()
            begin(t // step + plan.window)
        half = jnp.dot(lhs[t], psi[src[t]], preferred_element_type=jnp.float32).astype(jnp.bfloat16)
        acc[slot_of[t]] += lax.dot_general(
            half, rhs[t], (((1,), (1,)), ((), ())), preferred_element_type=jnp.float32
        )

    op, sec = lax.axis_index("op"), lax.axis_index("sec")
    core, place = op % 2, plan.place(op, sec)
    lane = lax.broadcasted_iota(jnp.int32, (LABEL_ROWS, blk), 1)
    tile = jnp.zeros((LABEL_ROWS, blk), jnp.float32)
    for j in range(plan.slots):
        tile = jnp.where(lane == j, labels[j].astype(jnp.float32), tile)
    tile = tile.astype(jnp.bfloat16)
    for m in range(plan.places):
        for rc in range(2):
            row = pl.multiple_of(((place ^ m) * 2 + (core ^ rc)) * plan.rows, plan.rows)
            for j in range(plan.slots):
                to = (rc * plan.slots + j) * plan.rows
                outs[m][pl.ds(to, plan.rows), :] = acc[j, pl.ds(row, plan.rows), :].astype(jnp.bfloat16)
        outs[m][pl.ds(2 * plan.slots * plan.rows, LABEL_ROWS), :] = tile


def contract(plan, fetch, source, target, left, right, vector):
    blk, terms = plan.blk, plan.terms
    height = 2 * plan.slots * plan.rows + LABEL_ROWS
    bf16 = jnp.bfloat16
    spaces = [pltpu.HBM, pltpu.HBM, *[pltpu.HBM if fetch else pltpu.VMEM] * 2, pltpu.HBM]
    arrays = [
        pltpu.with_memory_space_constraint(x, space)
        for x, space in zip((source, target, left, right, vector), spaces)
    ]
    out_shape = [pltpu.VMEM((height, blk), bf16)] * plan.places
    if fetch:
        out_shape += [pltpu.VMEM((terms, blk, blk), bf16)] * 2
    return pl.pallas_call(
        functools.partial(contract_kernel, plan, fetch),
        in_specs=[pl.BlockSpec(memory_space=space) for space in spaces],
        out_specs=[pl.BlockSpec(memory_space=pltpu.VMEM)] * len(out_shape),
        out_shape=out_shape,
        scratch_shapes=[
            pltpu.SMEM((terms,), jnp.int32),
            pltpu.SMEM((terms,), jnp.int32),
            pltpu.VMEM((plan.held, blk, blk), bf16),
            pltpu.VMEM((plan.slots, blk, blk), jnp.float32),
            pltpu.SMEM((terms,), jnp.int32),
            pltpu.SMEM((plan.slots,), jnp.int32),
            pltpu.SMEM((plan.sec,), jnp.int32),
            pltpu.SemaphoreType.DMA((2, terms // plan.step)),
            pltpu.SemaphoreType.DMA((3,)),
        ],
        cost_estimate=pl.CostEstimate(
            flops=4 * terms * blk**3,
            bytes_accessed=4 * terms * blk * blk if fetch else terms * blk,
            transcendentals=0,
        ),
        compiler_params=pltpu.CompilerParams(vmem_limit_bytes=VMEM_LIMIT),
        name="contract",
    )(*arrays)


def spread_kernel(plan, *refs):
    n = 2 * plan.places
    blocks, tags, outs = refs[:n], refs[n : 2 * n], refs[2 * n : 2 * n + 2]
    acc, tags_vector, tags_scalar, sem = refs[2 * n + 2 :]
    for i in range(n):
        row = jnp.max(tags[i][...].astype(jnp.float32), axis=0, keepdims=True)
        tags_vector[pl.ds(i, 1), :] = row[:, :128].astype(jnp.int32)
    copy = pltpu.make_async_copy(tags_vector, tags_scalar, sem)
    copy.start()
    acc[...] = jnp.zeros_like(acc)
    copy.wait()
    sec = lax.axis_index("sec")
    for i in range(n):
        for j in range(plan.slots):
            label = tags_scalar[i, j]
            away = (label // plan.held) ^ sec
            index = jnp.int32(0)
            for b in plan.bits:
                index = index * 2 + ((away >> b) & 1)
            index = index * 2 ** len(plan.inside) + plan.extra(away)
            acc[index * plan.held + label % plan.held] += blocks[i][pl.ds(j * plan.rows, plan.rows), :].astype(jnp.float32)
    half = acc.shape[0] // 2
    for k, out in enumerate(outs):
        out[...] = acc[pl.ds((1 - k) * half, half)].astype(jnp.bfloat16).reshape(out.shape)


def spread(plan, own, other):
    blk, rows, slots = plan.blk, plan.rows, plan.slots
    sectors = plan.held * plan.sec
    n = 2 * plan.places

    def half(rc):
        return pl.BlockSpec((slots * rows, blk), lambda t: (rc, 0))

    tag = pl.BlockSpec((LABEL_ROWS, blk), lambda t: (2 * slots * rows // LABEL_ROWS, 0))
    height = sectors // 2 * rows
    return pl.pallas_call(
        functools.partial(spread_kernel, plan),
        grid=(1,),
        in_specs=[half(0)] * plan.places + [half(1)] * plan.places + [tag] * n,
        out_specs=[pl.BlockSpec((height, blk), lambda t: (0, 0))] * 2,
        out_shape=[jax.ShapeDtypeStruct((height, blk), jnp.bfloat16)] * 2,
        scratch_shapes=[
            pltpu.VMEM((sectors, rows, blk), jnp.float32),
            pltpu.VMEM((n, 128), jnp.int32),
            pltpu.SMEM((n, 128), jnp.int32),
            pltpu.SemaphoreType.DMA,
        ],
        cost_estimate=pl.CostEstimate(flops=1, bytes_accessed=1, transcendentals=0),
        compiler_params=pltpu.CompilerParams(vmem_limit_bytes=VMEM_LIMIT),
        name="spread",
    )(*own, *other, *own, *other)


def place_kernel(plans, *refs):
    n = 2 * plans[0].places
    inputs, outs, sems = refs[: n * len(plans)], refs[n * len(plans) : -1], refs[-1]
    op, sec = lax.axis_index("op"), lax.axis_index("sec")
    moving = []
    for k, (plan, out) in enumerate(zip(plans, outs)):
        core, place = op % 2, plan.place(op, sec)
        for i, piece in enumerate(inputs[k * n : (k + 1) * n]):
            rc, m = divmod(i, plan.places)
            row = pl.multiple_of(((place ^ m) * 2 + (core ^ rc)) * plan.rows, plan.rows)
            moving.append(pltpu.make_async_copy(piece, out.at[:, pl.ds(row, plan.rows), :], sems.at[k, i]))
    for copy in moving:
        copy.start()
    for copy in moving:
        copy.wait()


def assemble(plans, gathered):
    plan = plans[0]
    pieces = [
        pltpu.with_memory_space_constraint(x.reshape(plan.held, plan.rows, plan.blk), pltpu.VMEM)
        for own, other in gathered
        for x in (*own, *other)
    ]
    return pl.pallas_call(
        functools.partial(place_kernel, plans),
        in_specs=[pl.BlockSpec(memory_space=pltpu.VMEM)] * len(pieces),
        out_specs=[pl.BlockSpec(memory_space=pl.ANY)] * len(plans),
        out_shape=[jax.ShapeDtypeStruct((plan.held, plan.blk, plan.blk), jnp.bfloat16)] * len(plans),
        scratch_shapes=[pltpu.SemaphoreType.DMA((len(plans), 2 * plan.places))],
        compiler_params=pltpu.CompilerParams(vmem_limit_bytes=VMEM_LIMIT),
        name="assemble",
    )(*pieces)


def across(plan, pieces):
    own = list(pieces)
    for m in reversed(range(1, plan.places)):
        own[m] = lax.ppermute(pieces[m], AXES, plan.across(m))
    return own


def to_core(plan, own):
    return [lax.ppermute(x, AXES, plan.swap(1, 0)) for x in own]


def add(arrived, kept):
    return kept.astype(jnp.float32) + arrived.astype(jnp.float32)


def halves(total):
    middle = total.shape[0] // 2
    return total[middle:].astype(jnp.bfloat16), total[:middle]


def gather(plan, total):
    total = total.astype(jnp.bfloat16)
    size = plan.held * plan.rows
    extras = 2 ** len(plan.inside)
    sums = [total[e * size : (e + 1) * size] for e in range(extras)]
    own = across(plan, [sums[m % extras] for m in range(plan.places)])
    return own, to_core(plan, own)


def per_device(mesh, first, second, left, right, source, target):
    terms = left.shape[0]
    order = list(range(mesh.shape["sec"].bit_length() - 1))
    plans = [
        Plan(mesh, first, terms, order),
        Plan(mesh, first, terms, [order[1], order[0], *order[2:]]),
    ]

    *pieces, lhs, rhs = contract(plans[0], True, source, target, left, right, first)
    early = across(plans[0], pieces)
    pieces = contract(plans[1], False, source, target, lhs, rhs, second)
    early, pieces = lax.optimization_barrier((early, pieces))
    late = across(plans[1], pieces)

    forwarded = to_core(plans[0], early)
    forwarded, late[-1] = lax.optimization_barrier((forwarded, late[-1]))
    away, kept = spread(plans[0], early, forwarded)
    arrived = lax.ppermute(away, AXES, plans[0].swap(0, 1 << plans[0].bits[0]))
    late_away, late_kept = spread(plans[1], late, to_core(plans[1], late))
    arrived, late_away = lax.optimization_barrier((arrived, late_away))
    late_arrived = lax.ppermute(late_away, AXES, plans[1].swap(0, 1 << plans[1].bits[0]))

    for k in range(1, len(plans[0].bits)):
        away, kept = halves(add(arrived, kept))
        arrived = lax.ppermute(away, AXES, plans[0].swap(0, 1 << plans[0].bits[k]))
        away, late_kept = halves(add(late_arrived, late_kept))
        arrived, away = lax.optimization_barrier((arrived, away))
        late_arrived = lax.ppermute(away, AXES, plans[1].swap(0, 1 << plans[1].bits[k]))
    totals = add(arrived, kept), add(late_arrived, late_kept)
    return tuple(assemble(plans, [gather(plan, total) for plan, total in zip(plans, totals)]))


def solution(mesh):
    in_specs = (
        P("sec", None, None),
        P("sec", None, None),
        P(AXES, None, None),
        P(AXES, None, None),
        P(AXES),
        P(AXES),
    )
    out_specs = (P("sec", None, None), P("sec", None, None))
    return jax.shard_map(
        functools.partial(per_device, mesh),
        mesh=mesh,
        in_specs=in_specs,
        out_specs=out_specs,
        check_vma=False,
    )
```

```python
import functools

import jax
import jax.numpy as jnp
from jax import lax
from jax.experimental import pallas as pl
from jax.experimental.pallas import tpu as pltpu
from jax.sharding import PartitionSpec as P

VMEM_LIMIT = 16 * 1024 * 1024
LABEL_ROWS = 16
AXES = ("op", "sec")


class Plan:
    def __init__(self, mesh, psi, terms, order):
        self.op, self.sec = mesh.shape["op"], mesh.shape["sec"]
        self.held, self.blk = psi.shape[0], psi.shape[1]
        self.terms = terms
        self.slots = self.sec // 2
        extra = 0
        while self.slots * self.op * 2**extra < self.held * self.sec:
            extra += 1
        self.inside, self.bits = order[:extra], order[extra:]
        self.places = (self.op // 2) * 2**extra
        self.rows = self.blk // (2 * self.places)
        self.step, self.window = 8, 2

    def extra(self, sec):
        total = sec * 0
        for i, b in enumerate(self.inside):
            total = total + (((sec >> b) & 1) << i)
        return total

    def place(self, op, sec):
        return (op // 2) * 2 ** len(self.inside) + self.extra(sec)

    def swap(self, op_mask, sec_mask):
        n = self.op * self.sec
        mask = op_mask * self.sec + sec_mask
        return [(i, i ^ mask) for i in range(n)]

    def across(self, m):
        sec_mask = sum(((m >> i) & 1) << b for i, b in enumerate(self.inside))
        return self.swap((m >> len(self.inside)) << 1, sec_mask)


def contract_kernel(plan, fetch, *refs):
    source, target, left, right, vector = refs[:5]
    outs, refs = refs[5 : 5 + plan.places], refs[5 + plan.places :]
    if fetch:
        lhs, rhs, refs = refs[0], refs[1], refs[2:]
    else:
        lhs, rhs = left, right
    src, tgt, psi, acc, slot_of, labels, seen, sems, first_sems = refs
    blk, terms, step = plan.blk, plan.terms, plan.step
    chunks = terms // step if fetch else 0

    heads = [
        pltpu.make_async_copy(x, y, first_sems.at[i])
        for i, (x, y) in enumerate(((target, tgt), (source, src), (vector, psi)))
    ]
    for copy in heads:
        copy.start()

    def loads(c):
        part = pl.ds(c * step, step)
        return [
            pltpu.make_async_copy(left.at[part], lhs.at[part], sems.at[0, c]),
            pltpu.make_async_copy(right.at[part], rhs.at[part], sems.at[1, c]),
        ]

    def begin(c):
        if c < chunks:
            for copy in loads(c):
                copy.start()

    for c in range(plan.window):
        begin(c)
    for h in range(plan.sec):
        seen[h] = -1
    acc[...] = jnp.zeros_like(acc)
    heads[0].wait()

    def name(t, count):
        goal = tgt[t]
        holder = goal // plan.held
        fresh = seen[holder] < 0
        slot = jnp.where(fresh, count, seen[holder])
        seen[holder] = slot
        labels[slot] = goal
        slot_of[t] = slot
        return count + fresh.astype(jnp.int32)

    lax.fori_loop(0, terms, name, jnp.int32(0))
    for copy in heads[1:]:
        copy.wait()

    for t in range(terms):
        if fetch and t % step == 0:
            for copy in loads(t // step):
                copy.wait()
            begin(t // step + plan.window)
        half = jnp.dot(lhs[t], psi[src[t]], preferred_element_type=jnp.float32).astype(jnp.bfloat16)
        acc[slot_of[t]] += lax.dot_general(
            half, rhs[t], (((1,), (1,)), ((), ())), preferred_element_type=jnp.float32
        )

    op, sec = lax.axis_index("op"), lax.axis_index("sec")
    core, place = op % 2, plan.place(op, sec)
    lane = lax.broadcasted_iota(jnp.int32, (LABEL_ROWS, blk), 1)
    tile = jnp.zeros((LABEL_ROWS, blk), jnp.float32)
    for j in range(plan.slots):
        tile = jnp.where(lane == j, labels[j].astype(jnp.float32), tile)
    tile = tile.astype(jnp.bfloat16)
    for m in range(plan.places):
        for rc in range(2):
            row = pl.multiple_of(((place ^ m) * 2 + (core ^ rc)) * plan.rows, plan.rows)
            for j in range(plan.slots):
                to = (rc * plan.slots + j) * plan.rows
                outs[m][pl.ds(to, plan.rows), :] = acc[j, pl.ds(row, plan.rows), :].astype(jnp.bfloat16)
        outs[m][pl.ds(2 * plan.slots * plan.rows, LABEL_ROWS), :] = tile


def contract(plan, fetch, source, target, left, right, vector):
    blk, terms = plan.blk, plan.terms
    height = 2 * plan.slots * plan.rows + LABEL_ROWS
    bf16 = jnp.bfloat16
    spaces = [pltpu.HBM, pltpu.HBM, *[pltpu.HBM if fetch else pltpu.VMEM] * 2, pltpu.HBM]
    arrays = [
        pltpu.with_memory_space_constraint(x, space)
        for x, space in zip((source, target, left, right, vector), spaces)
    ]
    out_shape = [pltpu.VMEM((height, blk), bf16)] * plan.places
    if fetch:
        out_shape += [pltpu.VMEM((terms, blk, blk), bf16)] * 2
    return pl.pallas_call(
        functools.partial(contract_kernel, plan, fetch),
        in_specs=[pl.BlockSpec(memory_space=space) for space in spaces],
        out_specs=[pl.BlockSpec(memory_space=pltpu.VMEM)] * len(out_shape),
        out_shape=out_shape,
        scratch_shapes=[
            pltpu.SMEM((terms,), jnp.int32),
            pltpu.SMEM((terms,), jnp.int32),
            pltpu.VMEM((plan.held, blk, blk), bf16),
            pltpu.VMEM((plan.slots, blk, blk), jnp.float32),
            pltpu.SMEM((terms,), jnp.int32),
            pltpu.SMEM((plan.slots,), jnp.int32),
            pltpu.SMEM((plan.sec,), jnp.int32),
            pltpu.SemaphoreType.DMA((2, terms // plan.step)),
            pltpu.SemaphoreType.DMA((3,)),
        ],
        cost_estimate=pl.CostEstimate(
            flops=4 * terms * blk**3,
            bytes_accessed=4 * terms * blk * blk if fetch else terms * blk,
            transcendentals=0,
        ),
        compiler_params=pltpu.CompilerParams(vmem_limit_bytes=VMEM_LIMIT),
        name="contract",
    )(*arrays)


def spread_kernel(plan, *refs):
    n = 2 * plan.places
    blocks, tags, outs = refs[:n], refs[n : 2 * n], refs[2 * n : 2 * n + 2]
    acc, tags_vector, tags_scalar, sem = refs[2 * n + 2 :]
    for i in range(n):
        row = jnp.max(tags[i][...].astype(jnp.float32), axis=0, keepdims=True)
        tags_vector[pl.ds(i, 1), :] = row[:, :128].astype(jnp.int32)
    copy = pltpu.make_async_copy(tags_vector, tags_scalar, sem)
    copy.start()
    acc[...] = jnp.zeros_like(acc)
    copy.wait()
    sec = lax.axis_index("sec")
    for i in range(n):
        for j in range(plan.slots):
            label = tags_scalar[i, j]
            away = (label // plan.held) ^ sec
            index = jnp.int32(0)
            for b in plan.bits:
                index = index * 2 + ((away >> b) & 1)
            index = index * 2 ** len(plan.inside) + plan.extra(away)
            acc[index * plan.held + label % plan.held] += blocks[i][pl.ds(j * plan.rows, plan.rows), :].astype(jnp.float32)
    half = acc.shape[0] // 2
    for k, out in enumerate(outs):
        out[...] = acc[pl.ds((1 - k) * half, half)].astype(jnp.bfloat16).reshape(out.shape)


def spread(plan, own, other):
    blk, rows, slots = plan.blk, plan.rows, plan.slots
    sectors = plan.held * plan.sec
    n = 2 * plan.places

    def half(rc):
        return pl.BlockSpec((slots * rows, blk), lambda t: (rc, 0))

    tag = pl.BlockSpec((LABEL_ROWS, blk), lambda t: (2 * slots * rows // LABEL_ROWS, 0))
    height = sectors // 2 * rows
    return pl.pallas_call(
        functools.partial(spread_kernel, plan),
        grid=(1,),
        in_specs=[half(0)] * plan.places + [half(1)] * plan.places + [tag] * n,
        out_specs=[pl.BlockSpec((height, blk), lambda t: (0, 0))] * 2,
        out_shape=[jax.ShapeDtypeStruct((height, blk), jnp.bfloat16)] * 2,
        scratch_shapes=[
            pltpu.VMEM((sectors, rows, blk), jnp.float32),
            pltpu.VMEM((n, 128), jnp.int32),
            pltpu.SMEM((n, 128), jnp.int32),
            pltpu.SemaphoreType.DMA,
        ],
        cost_estimate=pl.CostEstimate(flops=1, bytes_accessed=1, transcendentals=0),
        compiler_params=pltpu.CompilerParams(vmem_limit_bytes=VMEM_LIMIT),
        name="spread",
    )(*own, *other, *own, *other)


def place_kernel(plans, *refs):
    n = 2 * plans[0].places
    inputs, outs, sems = refs[: n * len(plans)], refs[n * len(plans) : -1], refs[-1]
    op, sec = lax.axis_index("op"), lax.axis_index("sec")
    moving = []
    for k, (plan, out) in enumerate(zip(plans, outs)):
        core, place = op % 2, plan.place(op, sec)
        for i, piece in enumerate(inputs[k * n : (k + 1) * n]):
            rc, m = divmod(i, plan.places)
            row = pl.multiple_of(((place ^ m) * 2 + (core ^ rc)) * plan.rows, plan.rows)
            moving.append(pltpu.make_async_copy(piece, out.at[:, pl.ds(row, plan.rows), :], sems.at[k, i]))
    for copy in moving:
        copy.start()
    for copy in moving:
        copy.wait()


def assemble(plans, gathered):
    plan = plans[0]
    pieces = [
        pltpu.with_memory_space_constraint(x.reshape(plan.held, plan.rows, plan.blk), pltpu.VMEM)
        for own, other in gathered
        for x in (*own, *other)
    ]
    return pl.pallas_call(
        functools.partial(place_kernel, plans),
        in_specs=[pl.BlockSpec(memory_space=pltpu.VMEM)] * len(pieces),
        out_specs=[pl.BlockSpec(memory_space=pl.ANY)] * len(plans),
        out_shape=[jax.ShapeDtypeStruct((plan.held, plan.blk, plan.blk), jnp.bfloat16)] * len(plans),
        scratch_shapes=[pltpu.SemaphoreType.DMA((len(plans), 2 * plan.places))],
        compiler_params=pltpu.CompilerParams(vmem_limit_bytes=VMEM_LIMIT),
        name="assemble",
    )(*pieces)


def across(plan, pieces):
    own = list(pieces)
    for m in reversed(range(1, plan.places)):
        own[m] = lax.ppermute(pieces[m], AXES, plan.across(m))
    return own


def to_core(plan, own):
    return [lax.ppermute(x, AXES, plan.swap(1, 0)) for x in own]


def after(x, y):
    return lax.optimization_barrier((x, y))[0]


def add(arrived, kept):
    return kept.astype(jnp.float32) + arrived.astype(jnp.float32)


def halves(total):
    middle = total.shape[0] // 2
    return total[middle:].astype(jnp.bfloat16), total[:middle]


def gather(plan, total):
    total = total.astype(jnp.bfloat16)
    size = plan.held * plan.rows
    extras = 2 ** len(plan.inside)
    sums = [total[e * size : (e + 1) * size] for e in range(extras)]
    own = across(plan, [sums[m % extras] for m in range(plan.places)])
    return own, to_core(plan, own)


def per_device(mesh, first, second, left, right, source, target):
    terms = left.shape[0]
    order = list(range(mesh.shape["sec"].bit_length() - 1))
    plans = [
        Plan(mesh, first, terms, order),
        Plan(mesh, first, terms, [order[1], order[0], *order[2:]]),
    ]

    *pieces, lhs, rhs = contract(plans[0], True, source, target, left, right, first)
    early = across(plans[0], pieces)
    pieces = contract(plans[1], False, source, target, lhs, rhs, second)
    early = after(early, pieces)
    late = across(plans[1], pieces)

    forwarded = to_core(plans[0], early)
    forwarded = after(forwarded, late[-1])
    away, kept = spread(plans[0], early, forwarded)
    arrived = lax.ppermute(away, AXES, plans[0].swap(0, 1 << plans[0].bits[0]))
    late = after(late, away)
    late_away, late_kept = spread(plans[1], late, to_core(plans[1], late))
    arrived = after(arrived, late_away)
    late_arrived = lax.ppermute(late_away, AXES, plans[1].swap(0, 1 << plans[1].bits[0]))

    for k in range(1, len(plans[0].bits)):
        away, kept = halves(add(arrived, kept))
        arrived = lax.ppermute(away, AXES, plans[0].swap(0, 1 << plans[0].bits[k]))
        away, late_kept = halves(add(late_arrived, late_kept))
        arrived = after(arrived, away)
        late_arrived = lax.ppermute(away, AXES, plans[1].swap(0, 1 << plans[1].bits[k]))
    totals = add(arrived, kept), add(late_arrived, late_kept)
    return tuple(assemble(plans, [gather(plan, total) for plan, total in zip(plans, totals)]))


def solution(mesh):
    in_specs = (
        P("sec", None, None),
        P("sec", None, None),
        P(AXES, None, None),
        P(AXES, None, None),
        P(AXES),
        P(AXES),
    )
    out_specs = (P("sec", None, None), P("sec", None, None))
    return jax.shard_map(
        functools.partial(per_device, mesh),
        mesh=mesh,
        in_specs=in_specs,
        out_specs=out_specs,
        check_vma=False,
    )
```

```python
import functools

import jax
import jax.numpy as jnp
from jax import lax
from jax.experimental import pallas as pl
from jax.experimental.pallas import tpu as pltpu
from jax.sharding import PartitionSpec as P

VMEM_LIMIT = 16 * 1024 * 1024
LABEL_ROWS = 16
AXES = ("op", "sec")


class Plan:
    def __init__(self, mesh, psi, terms):
        self.op, self.sec = mesh.shape["op"], mesh.shape["sec"]
        self.held, self.blk = psi.shape[0], psi.shape[1]
        self.terms = terms
        self.slots = self.sec // 2
        self.extra = 0
        while self.slots * self.op * 2**self.extra < self.held * self.sec:
            self.extra += 1
        order = list(range(self.sec.bit_length() - 1))
        orders = [order, [order[1], order[0], *order[2:]]]
        self.inside = [x[: self.extra] for x in orders]
        self.bits = [x[self.extra :] for x in orders]
        self.places = (self.op // 2) * 2**self.extra
        self.rows = self.blk // (2 * self.places)
        self.part = self.slots * self.rows
        self.step, self.window = 8, 2

    def inner(self, core, sec):
        total = sec * 0
        for i, b in enumerate(self.inside[core]):
            total = total + (((sec >> b) & 1) << i)
        return total

    def here(self):
        op, sec = lax.axis_index("op"), lax.axis_index("sec")
        core = op % 2
        first, second = ((op // 2) * 2**self.extra + self.inner(c, sec) for c in range(2))
        own = jnp.where(core == 0, first, second)
        return core, sec, own, first + second - own

    def row(self, place, core):
        return pl.multiple_of((place * 2 + core) * self.rows, self.rows)

    def partners(self, op_mask, sec_masks):
        pairs = []
        for op in range(self.op):
            for sec in range(self.sec):
                other = (op ^ op_mask) * self.sec + (sec ^ sec_masks[op % 2])
                pairs.append((op * self.sec + sec, other))
        return pairs

    def to_core(self, x):
        return lax.ppermute(x, AXES, self.partners(1, (0, 0)))

    def across(self, x, mask):
        if mask == 0:
            return x
        sec_masks = [sum(((mask >> i) & 1) << b for i, b in enumerate(inside)) for inside in self.inside]
        return lax.ppermute(x, AXES, self.partners((mask >> self.extra) << 1, sec_masks))

    def halve(self, k, x):
        return lax.ppermute(x, AXES, self.partners(0, [1 << bits[k] for bits in self.bits]))


def contract_kernel(plan, fetch, *refs):
    source, target, left, right, vector = refs[:5]
    keep, give, refs = refs[5], refs[6], refs[7:]
    if fetch:
        lhs, rhs, refs = refs[0], refs[1], refs[2:]
    else:
        lhs, rhs = left, right
    src, tgt, psi, acc, slot_of, labels, seen, sems, first_sems = refs
    blk, terms, step = plan.blk, plan.terms, plan.step
    chunks = terms // step if fetch else 0

    heads = [
        pltpu.make_async_copy(x, y, first_sems.at[i])
        for i, (x, y) in enumerate(((target, tgt), (source, src), (vector, psi)))
    ]
    for copy in heads:
        copy.start()

    def loads(c):
        part = pl.ds(c * step, step)
        return [
            pltpu.make_async_copy(left.at[part], lhs.at[part], sems.at[0, c]),
            pltpu.make_async_copy(right.at[part], rhs.at[part], sems.at[1, c]),
        ]

    def begin(c):
        if c < chunks:
            for copy in loads(c):
                copy.start()

    for c in range(plan.window):
        begin(c)
    for h in range(plan.sec):
        seen[h] = -1
    acc[...] = jnp.zeros_like(acc)
    heads[0].wait()

    def name(t, count):
        goal = tgt[t]
        holder = goal // plan.held
        fresh = seen[holder] < 0
        slot = jnp.where(fresh, count, seen[holder])
        seen[holder] = slot
        labels[slot] = goal
        slot_of[t] = slot
        return count + fresh.astype(jnp.int32)

    lax.fori_loop(0, terms, name, jnp.int32(0))
    for copy in heads[1:]:
        copy.wait()

    for t in range(terms):
        if fetch and t % step == 0:
            for copy in loads(t // step):
                copy.wait()
            begin(t // step + plan.window)
        half = jnp.dot(lhs[t], psi[src[t]], preferred_element_type=jnp.float32).astype(jnp.bfloat16)
        acc[slot_of[t]] += lax.dot_general(
            half, rhs[t], (((1,), (1,)), ((), ())), preferred_element_type=jnp.float32
        )

    core, _, place, other_place = plan.here()
    lane = lax.broadcasted_iota(jnp.int32, (LABEL_ROWS, blk), 1)
    tile = jnp.zeros((LABEL_ROWS, blk), jnp.float32)
    for j in range(plan.slots):
        tile = jnp.where(lane == core * plan.slots + j, labels[j].astype(jnp.float32), tile)
    tile = tile.astype(jnp.bfloat16)
    for m in range(plan.places):
        for out, row in ((keep, plan.row(place ^ m, core)), (give, plan.row(other_place ^ m, 1 - core))):
            for j in range(plan.slots):
                block = acc[j, pl.ds(row, plan.rows), :].astype(jnp.bfloat16)
                out[m, pl.ds(j * plan.rows, plan.rows), :] = block
            out[m, pl.ds(plan.part, LABEL_ROWS), :] = tile


def contract(plan, fetch, source, target, left, right, vector):
    blk, terms = plan.blk, plan.terms
    bf16 = jnp.bfloat16
    spaces = [pltpu.HBM, pltpu.HBM, *[pltpu.HBM if fetch else pltpu.VMEM] * 2, pltpu.HBM]
    arrays = [
        pltpu.with_memory_space_constraint(x, space)
        for x, space in zip((source, target, left, right, vector), spaces)
    ]
    out_shape = [pltpu.VMEM((plan.places, plan.part + LABEL_ROWS, blk), bf16)] * 2
    if fetch:
        out_shape += [pltpu.VMEM((terms, blk, blk), bf16)] * 2
    return pl.pallas_call(
        functools.partial(contract_kernel, plan, fetch),
        in_specs=[pl.BlockSpec(memory_space=space) for space in spaces],
        out_specs=[pl.BlockSpec(memory_space=pltpu.VMEM)] * len(out_shape),
        out_shape=out_shape,
        scratch_shapes=[
            pltpu.SMEM((terms,), jnp.int32),
            pltpu.SMEM((terms,), jnp.int32),
            pltpu.VMEM((plan.held, blk, blk), bf16),
            pltpu.VMEM((plan.slots, blk, blk), jnp.float32),
            pltpu.SMEM((terms,), jnp.int32),
            pltpu.SMEM((plan.slots,), jnp.int32),
            pltpu.SMEM((plan.sec,), jnp.int32),
            pltpu.SemaphoreType.DMA((2, terms // plan.step)),
            pltpu.SemaphoreType.DMA((3,)),
        ],
        cost_estimate=pl.CostEstimate(
            flops=4 * terms * blk**3,
            bytes_accessed=4 * terms * blk * blk if fetch else terms * blk,
            transcendentals=0,
        ),
        compiler_params=pltpu.CompilerParams(vmem_limit_bytes=VMEM_LIMIT),
        name="contract",
    )(*arrays)


def merge_kernel(plan, kept, got, *outs):
    part = plan.part
    for m, out in enumerate(outs):
        out[pl.ds(0, part), :] = kept[m, pl.ds(0, part), :]
        out[pl.ds(part, part), :] = got[m, pl.ds(0, part), :]
        tail = pl.ds(part, LABEL_ROWS)
        out[pl.ds(2 * part, LABEL_ROWS), :] = kept[m, tail, :] + got[m, tail, :]


def merge(plan, kept, got):
    whole = pl.BlockSpec(memory_space=pltpu.VMEM)
    return pl.pallas_call(
        functools.partial(merge_kernel, plan),
        in_specs=[whole] * 2,
        out_specs=[whole] * plan.places,
        out_shape=[pltpu.VMEM((2 * plan.part + LABEL_ROWS, plan.blk), jnp.bfloat16)] * plan.places,
        cost_estimate=pl.CostEstimate(flops=1, bytes_accessed=1, transcendentals=0),
        compiler_params=pltpu.CompilerParams(vmem_limit_bytes=VMEM_LIMIT),
        name="merge",
    )(*(pltpu.with_memory_space_constraint(x, pltpu.VMEM) for x in (kept, got)))


def spread_kernel(plan, *refs):
    n = plan.places
    blocks, outs = refs[:n], refs[n : n + 2]
    acc, spots_vector, spots, sem = refs[n + 2 :]
    core, sec, _, _ = plan.here()
    for i in range(n):
        tile = blocks[i][pl.ds(2 * plan.part, LABEL_ROWS), :].astype(jnp.float32)
        spots_vector[pl.ds(i, 1), :] = jnp.max(tile, axis=0, keepdims=True)[:, :128].astype(jnp.int32)
    labels = spots_vector[...]
    shift = plan.held.bit_length() - 1
    away = (labels >> shift) ^ sec
    by_core = []
    for c in range(2):
        index = labels * 0
        for b in plan.bits[c]:
            index = index * 2 + ((away >> b) & 1)
        by_core.append(index * 2**plan.extra + plan.inner(c, away))
    spots_vector[...] = jnp.where(core == 0, *by_core) * plan.held + (labels & (plan.held - 1))
    copy = pltpu.make_async_copy(spots_vector, spots, sem)
    copy.start()
    acc[...] = jnp.zeros_like(acc)
    copy.wait()
    for i in range(n):
        for h in range(2):
            for j in range(plan.slots):
                block = blocks[i][pl.ds(h * plan.part + j * plan.rows, plan.rows), :]
                acc[spots[i, (core ^ h) * plan.slots + j]] += block.astype(jnp.float32)
    half = acc.shape[0] // 2
    for k, out in enumerate(outs):
        out[...] = acc[pl.ds((1 - k) * half, half)].astype(jnp.bfloat16).reshape(out.shape)


def spread(plan, pieces):
    blk, rows = plan.blk, plan.rows
    sectors = plan.held * plan.sec
    whole = pl.BlockSpec(memory_space=pltpu.VMEM)
    return pl.pallas_call(
        functools.partial(spread_kernel, plan),
        in_specs=[whole] * len(pieces),
        out_specs=[whole] * 2,
        out_shape=[pltpu.VMEM((sectors // 2 * rows, blk), jnp.bfloat16)] * 2,
        scratch_shapes=[
            pltpu.VMEM((sectors, rows, blk), jnp.float32),
            pltpu.VMEM((plan.places, 128), jnp.int32),
            pltpu.SMEM((plan.places, 128), jnp.int32),
            pltpu.SemaphoreType.DMA,
        ],
        cost_estimate=pl.CostEstimate(flops=1, bytes_accessed=1, transcendentals=0),
        compiler_params=pltpu.CompilerParams(vmem_limit_bytes=VMEM_LIMIT),
        name="spread",
    )(*(pltpu.with_memory_space_constraint(x, pltpu.VMEM) for x in pieces))


def place_kernel(plan, *refs):
    n = 2 * plan.places
    inputs, outs, sems = refs[: 2 * n], refs[2 * n : -1], refs[-1]
    core, _, place, other_place = plan.here()
    moving = []
    for v, out in enumerate(outs):
        for m in range(plan.places):
            for h, row in enumerate((plan.row(place ^ m, core), plan.row(other_place ^ m, 1 - core))):
                i = h * plan.places + m
                part = out.at[:, pl.ds(row, plan.rows), :]
                moving.append(pltpu.make_async_copy(inputs[v * n + i], part, sems.at[v, i]))
    for copy in moving:
        copy.start()
    for copy in moving:
        copy.wait()


def assemble(plan, gathered):
    pieces = [
        pltpu.with_memory_space_constraint(x.reshape(plan.held, plan.rows, plan.blk), pltpu.VMEM)
        for pieces in gathered
        for x in pieces
    ]
    return pl.pallas_call(
        functools.partial(place_kernel, plan),
        in_specs=[pl.BlockSpec(memory_space=pltpu.VMEM)] * len(pieces),
        out_specs=[pl.BlockSpec(memory_space=pl.ANY)] * 2,
        out_shape=[jax.ShapeDtypeStruct((plan.held, plan.blk, plan.blk), jnp.bfloat16)] * 2,
        scratch_shapes=[pltpu.SemaphoreType.DMA((2, 2 * plan.places))],
        compiler_params=pltpu.CompilerParams(vmem_limit_bytes=VMEM_LIMIT),
        name="assemble",
    )(*pieces)


def after(x, y):
    return lax.optimization_barrier((x, y))[0]


def add(arrived, kept):
    return kept.astype(jnp.float32) + arrived.astype(jnp.float32)


def halves(total):
    middle = total.shape[0] // 2
    return total[middle:].astype(jnp.bfloat16), total[:middle]


def trade(plan, kept, given):
    pieces = merge(plan, kept, plan.to_core(given))
    return pieces, [plan.across(pieces[m], m) for m in range(plan.places)]


def gather(plan, total):
    total = total.astype(jnp.bfloat16)
    size = plan.held * plan.rows
    own = []
    for m in range(plan.places):
        inner = m % 2**plan.extra
        own.append(plan.across(total[inner * size : (inner + 1) * size], m))
    return own + [plan.to_core(x) for x in own]


def per_device(mesh, first, second, left, right, source, target):
    plan = Plan(mesh, first, left.shape[0])
    kept, given, lhs, rhs = contract(plan, True, source, target, left, right, first)
    pieces, early = trade(plan, kept, given)
    kept, given = contract(plan, False, after(source, pieces[-1]), target, lhs, rhs, second)
    early = after(early, kept)
    _, late = trade(plan, kept, after(given, early))

    away, kept = spread(plan, early)
    arrived = plan.halve(0, away)
    for k in range(1, len(plan.bits[0])):
        away, kept = halves(add(arrived, kept))
        arrived = plan.halve(k, away)

    late_away, late_kept = spread(plan, after(late, away))
    late_arrived = plan.halve(0, late_away)
    for k in range(1, len(plan.bits[0])):
        late_away, late_kept = halves(add(late_arrived, late_kept))
        late_arrived = plan.halve(k, late_away)
    return tuple(assemble(plan, [gather(plan, add(arrived, kept)), gather(plan, add(late_arrived, late_kept))]))


def solution(mesh):
    in_specs = (
        P("sec", None, None),
        P("sec", None, None),
        P(AXES, None, None),
        P(AXES, None, None),
        P(AXES),
        P(AXES),
    )
    out_specs = (P("sec", None, None), P("sec", None, None))
    return jax.shard_map(
        functools.partial(per_device, mesh),
        mesh=mesh,
        in_specs=in_specs,
        out_specs=out_specs,
        check_vma=False,
    )
```

```python
import functools

import jax
import jax.numpy as jnp
from jax import lax
from jax.experimental import pallas as pl
from jax.experimental.pallas import tpu as pltpu
from jax.sharding import PartitionSpec as P

VMEM_LIMIT = 16 * 1024 * 1024
LABEL_ROWS = 16
AXES = ("op", "sec")


class Plan:
    def __init__(self, mesh, psi, terms, swapped):
        self.op, self.sec = mesh.shape["op"], mesh.shape["sec"]
        self.held, self.blk = psi.shape[0], psi.shape[1]
        self.terms = terms
        self.slots = self.sec // 2
        self.extra = 0
        while self.slots * self.op * 2**self.extra < self.held * self.sec:
            self.extra += 1
        order = list(range(self.sec.bit_length() - 1))
        orders = [[order[1], order[0], *order[2:]] if swap else order for swap in swapped]
        self.inside = [x[: self.extra] for x in orders]
        self.bits = [x[self.extra :] for x in orders]
        self.places = (self.op // 2) * 2**self.extra
        self.rows = self.blk // (2 * self.places)
        self.part = self.slots * self.rows
        self.step, self.window = 8, 2

    def inner(self, core, sec):
        total = sec * 0
        for i, b in enumerate(self.inside[core]):
            total = total + (((sec >> b) & 1) << i)
        return total

    def here(self):
        op, sec = lax.axis_index("op"), lax.axis_index("sec")
        core = op % 2
        first, second = ((op // 2) * 2**self.extra + self.inner(c, sec) for c in range(2))
        own = jnp.where(core == 0, first, second)
        return core, sec, own, first + second - own

    def row(self, place, core):
        return pl.multiple_of((place * 2 + core) * self.rows, self.rows)

    def partners(self, op_mask, sec_masks):
        pairs = []
        for op in range(self.op):
            for sec in range(self.sec):
                other = (op ^ op_mask) * self.sec + (sec ^ sec_masks[op % 2])
                pairs.append((op * self.sec + sec, other))
        return pairs

    def to_core(self, x):
        return lax.ppermute(x, AXES, self.partners(1, (0, 0)))

    def across(self, x, mask):
        if mask == 0:
            return x
        sec_masks = [sum(((mask >> i) & 1) << b for i, b in enumerate(inside)) for inside in self.inside]
        return lax.ppermute(x, AXES, self.partners((mask >> self.extra) << 1, sec_masks))

    def halve(self, k, x):
        return lax.ppermute(x, AXES, self.partners(0, [1 << bits[k] for bits in self.bits]))


def contract_kernel(plan, fetch, *refs):
    source, target, left, right, vector = refs[:5]
    count = 2 if fetch else plan.places
    outs, refs = refs[5 : 5 + count], refs[5 + count :]
    if fetch:
        lhs, rhs, refs = refs[0], refs[1], refs[2:]
    else:
        lhs, rhs = left, right
    src, tgt, psi, acc, slot_of, labels, seen, sems, first_sems = refs
    blk, terms, step = plan.blk, plan.terms, plan.step
    chunks = terms // step if fetch else 0

    heads = [
        pltpu.make_async_copy(x, y, first_sems.at[i])
        for i, (x, y) in enumerate(((target, tgt), (source, src), (vector, psi)))
    ]
    for copy in heads:
        copy.start()

    def loads(c):
        part = pl.ds(c * step, step)
        return [
            pltpu.make_async_copy(left.at[part], lhs.at[part], sems.at[0, c]),
            pltpu.make_async_copy(right.at[part], rhs.at[part], sems.at[1, c]),
        ]

    def begin(c):
        if c < chunks:
            for copy in loads(c):
                copy.start()

    for c in range(plan.window):
        begin(c)
    for h in range(plan.sec):
        seen[h] = -1
    acc[...] = jnp.zeros_like(acc)
    heads[0].wait()

    def name(t, count):
        goal = tgt[t]
        holder = goal // plan.held
        fresh = seen[holder] < 0
        slot = jnp.where(fresh, count, seen[holder])
        seen[holder] = slot
        labels[slot] = goal
        slot_of[t] = slot
        return count + fresh.astype(jnp.int32)

    lax.fori_loop(0, terms, name, jnp.int32(0))
    for copy in heads[1:]:
        copy.wait()

    for t in range(terms):
        if fetch and t % step == 0:
            for copy in loads(t // step):
                copy.wait()
            begin(t // step + plan.window)
        half = jnp.dot(lhs[t], psi[src[t]], preferred_element_type=jnp.float32).astype(jnp.bfloat16)
        acc[slot_of[t]] += lax.dot_general(
            half, rhs[t], (((1,), (1,)), ((), ())), preferred_element_type=jnp.float32
        )

    core, _, place, other_place = plan.here()
    lane = lax.broadcasted_iota(jnp.int32, (LABEL_ROWS, blk), 1)
    tile = jnp.zeros((LABEL_ROWS, blk), jnp.float32)
    for j in range(plan.slots):
        tile = jnp.where(lane == core * plan.slots + j, labels[j].astype(jnp.float32), tile)
    tile = tile.astype(jnp.bfloat16)
    for m in range(plan.places):
        for h, row in enumerate((plan.row(place ^ m, core), plan.row(other_place ^ m, 1 - core))):
            out, base = (outs[h].at[m], 0) if fetch else (outs[m], h * plan.part)
            for j in range(plan.slots):
                block = acc[j, pl.ds(row, plan.rows), :].astype(jnp.bfloat16)
                out[pl.ds(base + j * plan.rows, plan.rows), :] = block
            if fetch or h == 1:
                out[pl.ds(base + plan.part, LABEL_ROWS), :] = tile


def contract(plan, fetch, source, target, left, right, vector):
    blk, terms = plan.blk, plan.terms
    bf16 = jnp.bfloat16
    spaces = [pltpu.HBM, pltpu.HBM, *[pltpu.HBM if fetch else pltpu.VMEM] * 2, pltpu.HBM]
    arrays = [
        pltpu.with_memory_space_constraint(x, space)
        for x, space in zip((source, target, left, right, vector), spaces)
    ]
    if fetch:
        out_shape = [pltpu.VMEM((plan.places, plan.part + LABEL_ROWS, blk), bf16)] * 2
        out_shape += [pltpu.VMEM((terms, blk, blk), bf16)] * 2
    else:
        out_shape = [pltpu.VMEM((2 * plan.part + LABEL_ROWS, blk), bf16)] * plan.places
    return pl.pallas_call(
        functools.partial(contract_kernel, plan, fetch),
        in_specs=[pl.BlockSpec(memory_space=space) for space in spaces],
        out_specs=[pl.BlockSpec(memory_space=pltpu.VMEM)] * len(out_shape),
        out_shape=out_shape,
        scratch_shapes=[
            pltpu.SMEM((terms,), jnp.int32),
            pltpu.SMEM((terms,), jnp.int32),
            pltpu.VMEM((plan.held, blk, blk), bf16),
            pltpu.VMEM((plan.slots, blk, blk), jnp.float32),
            pltpu.SMEM((terms,), jnp.int32),
            pltpu.SMEM((plan.slots,), jnp.int32),
            pltpu.SMEM((plan.sec,), jnp.int32),
            pltpu.SemaphoreType.DMA((2, terms // plan.step)),
            pltpu.SemaphoreType.DMA((3,)),
        ],
        cost_estimate=pl.CostEstimate(
            flops=4 * terms * blk**3,
            bytes_accessed=4 * terms * blk * blk if fetch else terms * blk,
            transcendentals=0,
        ),
        compiler_params=pltpu.CompilerParams(vmem_limit_bytes=VMEM_LIMIT),
        name="contract",
    )(*arrays)


def merge_kernel(plan, kept, got, *outs):
    part = plan.part
    for m, out in enumerate(outs):
        out[pl.ds(0, part), :] = kept[m, pl.ds(0, part), :]
        out[pl.ds(part, part), :] = got[m, pl.ds(0, part), :]
        tail = pl.ds(part, LABEL_ROWS)
        out[pl.ds(2 * part, LABEL_ROWS), :] = kept[m, tail, :] + got[m, tail, :]


def merge(plan, kept, got):
    whole = pl.BlockSpec(memory_space=pltpu.VMEM)
    return pl.pallas_call(
        functools.partial(merge_kernel, plan),
        in_specs=[whole] * 2,
        out_specs=[whole] * plan.places,
        out_shape=[pltpu.VMEM((2 * plan.part + LABEL_ROWS, plan.blk), jnp.bfloat16)] * plan.places,
        cost_estimate=pl.CostEstimate(flops=1, bytes_accessed=1, transcendentals=0),
        compiler_params=pltpu.CompilerParams(vmem_limit_bytes=VMEM_LIMIT),
        name="merge",
    )(*(pltpu.with_memory_space_constraint(x, pltpu.VMEM) for x in (kept, got)))


def spread_kernel(plan, parts, *refs):
    n = 1 + max(i for i, _ in parts)
    blocks, outs = refs[:n], refs[n : n + 2]
    acc, spots_vector, spots, sem = refs[n + 2 :]
    core, sec, _, _ = plan.here()
    for i in range(n):
        tile = blocks[i][pl.ds(2 * plan.part, LABEL_ROWS), :].astype(jnp.float32)
        spots_vector[pl.ds(i, 1), :] = jnp.max(tile, axis=0, keepdims=True)[:, :128].astype(jnp.int32)
    labels = spots_vector[...]
    shift = plan.held.bit_length() - 1
    away = (labels >> shift) ^ sec
    by_core = []
    for c in range(2):
        index = labels * 0
        for b in plan.bits[c]:
            index = index * 2 + ((away >> b) & 1)
        by_core.append(index * 2**plan.extra + plan.inner(c, away))
    spots_vector[...] = jnp.where(core == 0, *by_core) * plan.held + (labels & (plan.held - 1))
    copy = pltpu.make_async_copy(spots_vector, spots, sem)
    copy.start()
    acc[...] = jnp.zeros_like(acc)
    copy.wait()
    for i, h in parts:
        for j in range(plan.slots):
            block = blocks[i][pl.ds(h * plan.part + j * plan.rows, plan.rows), :]
            acc[spots[i, (core ^ h) * plan.slots + j]] += block.astype(jnp.float32)
    half = acc.shape[0] // 2
    for k, out in enumerate(outs):
        out[...] = acc[pl.ds((1 - k) * half, half)].astype(jnp.bfloat16).reshape(out.shape)


def spread(plan, pieces, parts, weight):
    blk, rows = plan.blk, plan.rows
    sectors = plan.held * plan.sec
    whole = pl.BlockSpec(memory_space=pltpu.VMEM)
    return pl.pallas_call(
        functools.partial(spread_kernel, plan, parts),
        in_specs=[whole] * len(pieces),
        out_specs=[whole] * 2,
        out_shape=[pltpu.VMEM((sectors // 2 * rows, blk), jnp.bfloat16)] * 2,
        scratch_shapes=[
            pltpu.VMEM((sectors, rows, blk), jnp.float32),
            pltpu.VMEM((len(pieces), 128), jnp.int32),
            pltpu.SMEM((len(pieces), 128), jnp.int32),
            pltpu.SemaphoreType.DMA,
        ],
        cost_estimate=pl.CostEstimate(flops=1, bytes_accessed=weight, transcendentals=0),
        compiler_params=pltpu.CompilerParams(vmem_limit_bytes=VMEM_LIMIT),
        name="spread",
    )(*(pltpu.with_memory_space_constraint(x, pltpu.VMEM) for x in pieces))


def place_kernel(plans, *refs):
    n = 2 * plans[0].places
    inputs, outs, sems = refs[: 2 * n], refs[2 * n : -1], refs[-1]
    moving = []
    for v, (plan, out) in enumerate(zip(plans, outs)):
        core, _, place, other_place = plan.here()
        for m in range(plan.places):
            for h, row in enumerate((plan.row(place ^ m, core), plan.row(other_place ^ m, 1 - core))):
                i = h * plan.places + m
                part = out.at[:, pl.ds(row, plan.rows), :]
                moving.append(pltpu.make_async_copy(inputs[v * n + i], part, sems.at[v, i]))
    for copy in moving:
        copy.start()
    for copy in moving:
        copy.wait()


def assemble(plans, gathered):
    plan = plans[0]
    pieces = [
        pltpu.with_memory_space_constraint(x.reshape(plan.held, plan.rows, plan.blk), pltpu.VMEM)
        for pieces in gathered
        for x in pieces
    ]
    return pl.pallas_call(
        functools.partial(place_kernel, plans),
        in_specs=[pl.BlockSpec(memory_space=pltpu.VMEM)] * len(pieces),
        out_specs=[pl.BlockSpec(memory_space=pl.ANY)] * 2,
        out_shape=[jax.ShapeDtypeStruct((plan.held, plan.blk, plan.blk), jnp.bfloat16)] * 2,
        scratch_shapes=[pltpu.SemaphoreType.DMA((2, 2 * plan.places))],
        compiler_params=pltpu.CompilerParams(vmem_limit_bytes=VMEM_LIMIT),
        name="assemble",
    )(*pieces)


def after(x, y):
    return lax.optimization_barrier((x, y))[0]


def add(arrived, kept):
    return kept.astype(jnp.float32) + arrived.astype(jnp.float32)


def halves(total):
    middle = total.shape[0] // 2
    return total[middle:].astype(jnp.bfloat16), total[:middle]


def trade(plan, pieces):
    return [plan.across(x, m) for m, x in enumerate(pieces)]


def gather(plan, total):
    total = total.astype(jnp.bfloat16)
    size = plan.held * plan.rows
    own = []
    for m in range(plan.places):
        inner = m % 2**plan.extra
        own.append(plan.across(total[inner * size : (inner + 1) * size], m))
    return own + [plan.to_core(x) for x in own]


def per_device(mesh, first, second, left, right, source, target):
    plan = Plan(mesh, first, left.shape[0], (False, True))
    late_plan = Plan(mesh, first, left.shape[0], (True, True))
    places = range(plan.places)

    kept, given, lhs, rhs = contract(plan, True, source, target, left, right, first)
    merged = merge(plan, kept, plan.to_core(given))
    early = trade(plan, merged)
    pieces = contract(late_plan, False, after(source, merged[-1]), target, lhs, rhs, second)
    early = after(early, pieces)
    late = trade(late_plan, pieces)

    away, kept = spread(plan, early, [(m, h) for m in places for h in range(2)], 3000000)
    arrived = plan.halve(0, away)
    late = late[:1] + after(late[1:], away)
    parts = [(h * plan.places + m, h) for h in range(2) for m in places]
    late_away, late_kept = spread(late_plan, late + [late_plan.to_core(x) for x in late], parts, 100000000)
    arrived = after(arrived, late_away)
    late_arrived = late_plan.halve(0, late_away)

    for k in range(1, len(plan.bits[0])):
        away, kept = halves(add(arrived, kept))
        arrived = plan.halve(k, away)
        away, late_kept = halves(add(late_arrived, late_kept))
        arrived = after(arrived, away)
        late_arrived = late_plan.halve(k, away)
    gathered = gather(plan, add(arrived, kept)), gather(late_plan, add(late_arrived, late_kept))
    return tuple(assemble((plan, late_plan), gathered))


def solution(mesh):
    in_specs = (
        P("sec", None, None),
        P("sec", None, None),
        P(AXES, None, None),
        P(AXES, None, None),
        P(AXES),
        P(AXES),
    )
    out_specs = (P("sec", None, None), P("sec", None, None))
    return jax.shard_map(
        functools.partial(per_device, mesh),
        mesh=mesh,
        in_specs=in_specs,
        out_specs=out_specs,
        check_vma=False,
    )
```

```python
import functools

import jax
import jax.numpy as jnp
from jax import lax
from jax.experimental import pallas as pl
from jax.experimental.pallas import tpu as pltpu
from jax.sharding import PartitionSpec as P

VMEM_LIMIT = 16 * 1024 * 1024
LABEL_ROWS = 16
AXES = ("op", "sec")


class Plan:
    def __init__(self, mesh, psi, terms, swapped):
        self.op, self.sec = mesh.shape["op"], mesh.shape["sec"]
        self.held, self.blk = psi.shape[0], psi.shape[1]
        self.terms = terms
        self.slots = self.sec // 2
        self.extra = 0
        while self.slots * self.op * 2**self.extra < self.held * self.sec:
            self.extra += 1
        order = list(range(self.sec.bit_length() - 1))
        orders = [[order[1], order[0], *order[2:]] if swap else order for swap in swapped]
        self.inside = [x[: self.extra] for x in orders]
        self.bits = [x[self.extra :] for x in orders]
        self.places = (self.op // 2) * 2**self.extra
        self.rows = self.blk // (2 * self.places)
        self.part = self.slots * self.rows
        self.step, self.window = 8, 2

    def inner(self, core, sec):
        total = sec * 0
        for i, b in enumerate(self.inside[core]):
            total = total + (((sec >> b) & 1) << i)
        return total

    def here(self):
        op, sec = lax.axis_index("op"), lax.axis_index("sec")
        core = op % 2
        first, second = ((op // 2) * 2**self.extra + self.inner(c, sec) for c in range(2))
        own = jnp.where(core == 0, first, second)
        return core, sec, own, first + second - own

    def row(self, place, core):
        return pl.multiple_of((place * 2 + core) * self.rows, self.rows)

    def partners(self, op_mask, sec_masks):
        pairs = []
        for op in range(self.op):
            for sec in range(self.sec):
                other = (op ^ op_mask) * self.sec + (sec ^ sec_masks[op % 2])
                pairs.append((op * self.sec + sec, other))
        return pairs

    def to_core(self, x):
        return lax.ppermute(x, AXES, self.partners(1, (0, 0)))

    def across(self, x, mask):
        if mask == 0:
            return x
        sec_masks = [sum(((mask >> i) & 1) << b for i, b in enumerate(inside)) for inside in self.inside]
        return lax.ppermute(x, AXES, self.partners((mask >> self.extra) << 1, sec_masks))

    def halve(self, k, x):
        return lax.ppermute(x, AXES, self.partners(0, [1 << bits[k] for bits in self.bits]))


def contract_kernel(plan, fetch, *refs):
    blk, terms, step = plan.blk, plan.terms, plan.step
    if fetch:
        source, target, left, right, vector, later, *refs = refs
    else:
        notes, lhs, rhs, psi, *refs = refs
    count = 2 if fetch else plan.places
    outs, refs = refs[:count], refs[count:]
    if fetch:
        notes, lhs, rhs, psi_out, *refs = refs
        tgt, src, seen, psi, sems, first_sems, *refs = refs
    table, acc, sem = refs
    chunks = terms // step if fetch else 0
    acc[...] = jnp.zeros_like(acc)

    if fetch:
        heads = [
            pltpu.make_async_copy(x, y, first_sems.at[i])
            for i, (x, y) in enumerate(((target, tgt), (source, src), (vector, psi)))
        ]
        tail = pltpu.make_async_copy(later, psi_out, first_sems.at[3])
        for copy in heads:
            copy.start()

    def loads(c):
        part = pl.ds(c * step, step)
        return [
            pltpu.make_async_copy(left.at[part], lhs.at[part], sems.at[0, c]),
            pltpu.make_async_copy(right.at[part], rhs.at[part], sems.at[1, c]),
        ]

    def begin(c):
        if c < chunks:
            for copy in loads(c):
                copy.start()
        elif c == chunks:
            tail.start()

    def name(t, count):
        goal = tgt[t]
        holder = goal // plan.held
        fresh = seen[holder] < 0
        slot = jnp.where(fresh, count, seen[holder])
        seen[holder] = slot
        table[2, slot] = goal
        table[1, t] = slot
        table[0, t] = src[t]
        return count + fresh.astype(jnp.int32)

    if fetch:
        for c in range(plan.window):
            begin(c)
        for h in range(plan.sec):
            seen[h] = -1
        heads[0].wait()
        heads[1].wait()
        lax.fori_loop(0, terms, name, jnp.int32(0))
        heads[2].wait()
        copy = pltpu.make_async_copy(table, notes, sem)
        copy.start()
    else:
        copy = pltpu.make_async_copy(notes, table, sem)
        copy.start()
        copy.wait()

    for t in range(terms):
        if fetch and t % step == 0:
            for part in loads(t // step):
                part.wait()
            begin(t // step + plan.window)
        half = jnp.dot(lhs[t], psi[table[0, t]], preferred_element_type=jnp.float32).astype(jnp.bfloat16)
        acc[table[1, t]] += lax.dot_general(
            half, rhs[t], (((1,), (1,)), ((), ())), preferred_element_type=jnp.float32
        )

    core, _, place, other_place = plan.here()
    lane = lax.broadcasted_iota(jnp.int32, (LABEL_ROWS, blk), 1)
    tile = jnp.zeros((LABEL_ROWS, blk), jnp.float32)
    for j in range(plan.slots):
        tile = jnp.where(lane == core * plan.slots + j, table[2, j].astype(jnp.float32), tile)
    tile = tile.astype(jnp.bfloat16)
    for m in range(plan.places):
        for h, row in enumerate((plan.row(place ^ m, core), plan.row(other_place ^ m, 1 - core))):
            out, base = (outs[h].at[m], 0) if fetch else (outs[m], h * plan.part)
            for j in range(plan.slots):
                block = acc[j, pl.ds(row, plan.rows), :].astype(jnp.bfloat16)
                out[pl.ds(base + j * plan.rows, plan.rows), :] = block
            if fetch or h == 1:
                out[pl.ds(base + plan.part, LABEL_ROWS), :] = tile
    if fetch:
        copy.wait()
        tail.wait()


def contract(plan, fetch, *arrays):
    blk, terms = plan.blk, plan.terms
    bf16 = jnp.bfloat16
    space = pltpu.HBM if fetch else pltpu.VMEM
    scratch = [
        pltpu.SMEM((8, 128), jnp.int32),
        pltpu.VMEM((plan.slots, blk, blk), jnp.float32),
        pltpu.SemaphoreType.DMA,
    ]
    if fetch:
        out_shape = [pltpu.VMEM((plan.places, plan.part + LABEL_ROWS, blk), bf16)] * 2
        out_shape += [
            pltpu.VMEM((8, 128), jnp.int32),
            *[pltpu.VMEM((terms, blk, blk), bf16)] * 2,
            pltpu.VMEM((plan.held, blk, blk), bf16),
        ]
        scratch = [
            pltpu.SMEM((terms,), jnp.int32),
            pltpu.SMEM((terms,), jnp.int32),
            pltpu.SMEM((plan.sec,), jnp.int32),
            pltpu.VMEM((plan.held, blk, blk), bf16),
            pltpu.SemaphoreType.DMA((2, terms // plan.step)),
            pltpu.SemaphoreType.DMA((4,)),
        ] + scratch
    else:
        out_shape = [pltpu.VMEM((2 * plan.part + LABEL_ROWS, blk), bf16)] * plan.places
    return pl.pallas_call(
        functools.partial(contract_kernel, plan, fetch),
        in_specs=[pl.BlockSpec(memory_space=space)] * len(arrays),
        out_specs=[pl.BlockSpec(memory_space=pltpu.VMEM)] * len(out_shape),
        out_shape=out_shape,
        scratch_shapes=scratch,
        cost_estimate=pl.CostEstimate(
            flops=4 * terms * blk**3,
            bytes_accessed=4 * terms * blk * blk if fetch else terms * blk,
            transcendentals=0,
        ),
        compiler_params=pltpu.CompilerParams(vmem_limit_bytes=VMEM_LIMIT),
        name="contract",
    )(*(pltpu.with_memory_space_constraint(x, space) for x in arrays))


def merge_kernel(plan, kept, got, *outs):
    part = plan.part
    for m, out in enumerate(outs):
        out[pl.ds(0, part), :] = kept[m, pl.ds(0, part), :]
        out[pl.ds(part, part), :] = got[m, pl.ds(0, part), :]
        tail = pl.ds(part, LABEL_ROWS)
        out[pl.ds(2 * part, LABEL_ROWS), :] = kept[m, tail, :] + got[m, tail, :]


def merge(plan, kept, got):
    whole = pl.BlockSpec(memory_space=pltpu.VMEM)
    return pl.pallas_call(
        functools.partial(merge_kernel, plan),
        in_specs=[whole] * 2,
        out_specs=[whole] * plan.places,
        out_shape=[pltpu.VMEM((2 * plan.part + LABEL_ROWS, plan.blk), jnp.bfloat16)] * plan.places,
        cost_estimate=pl.CostEstimate(flops=1, bytes_accessed=1, transcendentals=0),
        compiler_params=pltpu.CompilerParams(vmem_limit_bytes=VMEM_LIMIT),
        name="merge",
    )(*(pltpu.with_memory_space_constraint(x, pltpu.VMEM) for x in (kept, got)))


def spread_kernel(plan, parts, *refs):
    n = 1 + max(i for i, _ in parts)
    blocks, outs = refs[:n], refs[n : n + 2]
    acc, spots_vector, spots, sem = refs[n + 2 :]
    core, sec, _, _ = plan.here()
    for i in range(n):
        tile = blocks[i][pl.ds(2 * plan.part, LABEL_ROWS), :].astype(jnp.float32)
        spots_vector[pl.ds(i, 1), :] = jnp.max(tile, axis=0, keepdims=True)[:, :128].astype(jnp.int32)
    labels = spots_vector[...]
    shift = plan.held.bit_length() - 1
    away = (labels >> shift) ^ sec
    by_core = []
    for c in range(2):
        index = labels * 0
        for b in plan.bits[c]:
            index = index * 2 + ((away >> b) & 1)
        by_core.append(index * 2**plan.extra + plan.inner(c, away))
    spots_vector[...] = jnp.where(core == 0, *by_core) * plan.held + (labels & (plan.held - 1))
    copy = pltpu.make_async_copy(spots_vector, spots, sem)
    copy.start()
    acc[...] = jnp.zeros_like(acc)
    copy.wait()
    for i, h in parts:
        for j in range(plan.slots):
            block = blocks[i][pl.ds(h * plan.part + j * plan.rows, plan.rows), :]
            acc[spots[i, (core ^ h) * plan.slots + j]] += block.astype(jnp.float32)
    half = acc.shape[0] // 2
    for k, out in enumerate(outs):
        out[...] = acc[pl.ds((1 - k) * half, half)].astype(jnp.bfloat16).reshape(out.shape)


def spread(plan, pieces, parts, weight):
    blk, rows = plan.blk, plan.rows
    sectors = plan.held * plan.sec
    whole = pl.BlockSpec(memory_space=pltpu.VMEM)
    return pl.pallas_call(
        functools.partial(spread_kernel, plan, parts),
        in_specs=[whole] * len(pieces),
        out_specs=[whole] * 2,
        out_shape=[pltpu.VMEM((sectors // 2 * rows, blk), jnp.bfloat16)] * 2,
        scratch_shapes=[
            pltpu.VMEM((sectors, rows, blk), jnp.float32),
            pltpu.VMEM((len(pieces), 128), jnp.int32),
            pltpu.SMEM((len(pieces), 128), jnp.int32),
            pltpu.SemaphoreType.DMA,
        ],
        cost_estimate=pl.CostEstimate(flops=1, bytes_accessed=weight, transcendentals=0),
        compiler_params=pltpu.CompilerParams(vmem_limit_bytes=VMEM_LIMIT),
        name="spread",
    )(*(pltpu.with_memory_space_constraint(x, pltpu.VMEM) for x in pieces))


def place_kernel(plans, *refs):
    n = 2 * plans[0].places
    inputs, outs, sems = refs[: 2 * n], refs[2 * n : -1], refs[-1]
    moving = []
    for v, (plan, out) in enumerate(zip(plans, outs)):
        core, _, place, other_place = plan.here()
        for m in range(plan.places):
            for h, row in enumerate((plan.row(place ^ m, core), plan.row(other_place ^ m, 1 - core))):
                i = h * plan.places + m
                part = out.at[:, pl.ds(row, plan.rows), :]
                moving.append(pltpu.make_async_copy(inputs[v * n + i], part, sems.at[v, i]))
    for copy in moving:
        copy.start()
    for copy in moving:
        copy.wait()


def assemble(plans, gathered):
    plan = plans[0]
    pieces = [
        pltpu.with_memory_space_constraint(x.reshape(plan.held, plan.rows, plan.blk), pltpu.VMEM)
        for pieces in gathered
        for x in pieces
    ]
    return pl.pallas_call(
        functools.partial(place_kernel, plans),
        in_specs=[pl.BlockSpec(memory_space=pltpu.VMEM)] * len(pieces),
        out_specs=[pl.BlockSpec(memory_space=pl.ANY)] * 2,
        out_shape=[jax.ShapeDtypeStruct((plan.held, plan.blk, plan.blk), jnp.bfloat16)] * 2,
        scratch_shapes=[pltpu.SemaphoreType.DMA((2, 2 * plan.places))],
        compiler_params=pltpu.CompilerParams(vmem_limit_bytes=VMEM_LIMIT),
        name="assemble",
    )(*pieces)


def after(x, y):
    return lax.optimization_barrier((x, y))[0]


def add(arrived, kept):
    return kept.astype(jnp.float32) + arrived.astype(jnp.float32)


def halves(total):
    middle = total.shape[0] // 2
    return total[middle:].astype(jnp.bfloat16), total[:middle]


def trade(plan, pieces):
    return [plan.across(x, m) for m, x in enumerate(pieces)]


def gather(plan, total):
    total = total.astype(jnp.bfloat16)
    size = plan.held * plan.rows
    own = []
    for m in range(plan.places):
        inner = m % 2**plan.extra
        own.append(plan.across(total[inner * size : (inner + 1) * size], m))
    return own + [plan.to_core(x) for x in own]


def per_device(mesh, first, second, left, right, source, target):
    plan = Plan(mesh, first, left.shape[0], (False, True))
    late_plan = Plan(mesh, first, left.shape[0], (True, True))
    places = range(plan.places)

    kept, given, notes, *operands = contract(plan, True, source, target, left, right, first, second)
    merged = merge(plan, kept, plan.to_core(given))
    early = trade(plan, merged)
    pieces = contract(late_plan, False, after(notes, merged[-1]), *operands)
    early = after(early, pieces)
    late = trade(late_plan, pieces)

    away, kept = spread(plan, early, [(m, h) for m in places for h in range(2)], 3000000)
    arrived = plan.halve(0, away)
    late = late[:1] + [after(x, away) for x in late[1:]]
    parts = [(h * plan.places + m, h) for h in range(2) for m in places]
    late_away, late_kept = spread(late_plan, late + [late_plan.to_core(x) for x in late], parts, 100000000)
    arrived = after(arrived, late_away)
    late_arrived = late_plan.halve(0, late_away)

    for k in range(1, len(plan.bits[0])):
        away, kept = halves(add(arrived, kept))
        arrived = plan.halve(k, away)
        away, late_kept = halves(add(late_arrived, late_kept))
        arrived = after(arrived, away)
        late_arrived = late_plan.halve(k, away)
    gathered = gather(plan, add(arrived, kept)), gather(late_plan, add(late_arrived, late_kept))
    return tuple(assemble((plan, late_plan), gathered))


def solution(mesh):
    in_specs = (
        P("sec", None, None),
        P("sec", None, None),
        P(AXES, None, None),
        P(AXES, None, None),
        P(AXES),
        P(AXES),
    )
    out_specs = (P("sec", None, None), P("sec", None, None))
    return jax.shard_map(
        functools.partial(per_device, mesh),
        mesh=mesh,
        in_specs=in_specs,
        out_specs=out_specs,
        check_vma=False,
    )
```
